512 devices in a mesh: row: 16 (over z_lo, x), col: 8 (over y, core), day: 4 (over z_hi).
Axes of the slice: x: 4, y: 4, z: 16 (z_hi: 4, z_lo: 4; z = z_hi * 4 + z_lo), core: 2. Of those that a mesh axis runs over, the one named last changes fastest.
Arguments:
- noise: bfloat16 [4, 8, 4096, 1500], P('day', 'col', 'row'), may hold values from -25 to 25
- keep: int32 [4, 8, 4096], P('day', 'col', 'row'), may hold values 0 or 1
Outputs:
- stacked: float32 [128, 51, 4096], P(('col', 'day'), None, 'row')
The draws below stay inside these ranges and needn't reach their ends.
All inputs are finite; a program needn't handle non-finite values. No bound on the sum of `keep` on one device may be relied on, other than what follows from the above.
Results may differ from the reference program's by a relative error of at most 0.02.
Values may be sent and summed in bfloat16 or wider, within the bound.
A program may use at most 64 MiB of HBM per device.

```python
import math
import jax
import jax.numpy as jnp
from jax import lax

C = 4096
TLEN = 1500
F = 256
LOW = 60
HALF = 64
MAXLAG = 25
LAGS = 51
WIN = 8
SRC = 128
DAYS = 4


def draw_noise(key, part):
    key = jax.random.fold_in(key, 7)
    key_scale, key_tap, key_base, key_common = jax.random.split(key, 4)
    full_shape = (DAYS, WIN, C, TLEN + 1)
    common_shape = (DAYS, WIN, 1, TLEN + 1)
    scales = jnp.exp(jax.random.uniform(key_scale, (C, 1), jnp.float32, math.log(0.3), math.log(3.0)))
    base_noise = jax.random.truncated_normal(key_base, -4.0, 4.0, full_shape, jnp.float32)
    common_noise = jax.random.truncated_normal(key_common, -4.0, 4.0, common_shape, jnp.float32)
    mixing = 0.15
    tap_gain = jax.random.uniform(key_tap, (C, 1), jnp.float32, -0.8, 0.8)
    combined = base_noise + mixing * common_noise
    return (scales * (combined[..., 1:] + tap_gain * combined[..., :-1])).astype(jnp.bfloat16)


def set_ends(array, own_key, low, high):
    dims = array.shape
    spot = [jax.random.randint(jax.random.fold_in(own_key, axis), (), 0, dims[axis]) for axis in range(len(dims))]
    array = array.at[tuple(spot)].set(low)
    longest = dims.index(max(dims))
    spot[longest] = (spot[longest] + 1) % dims[longest]
    return array.at[tuple(spot)].set(high)


def setup_inputs(seed: int = 0) -> dict:
    key_list = jax.random.split(jax.random.key(seed), 3)
    return {
        "noise": draw_noise(jax.random.fold_in(key_list[2], 71), 0),
        "keep": set_ends((jax.random.randint(key_list[1], (DAYS, WIN, C), 0, 2) < 1).astype(jnp.int32), jax.random.fold_in(key_list[1], 1), 0, 1),
    }


def reference(noise, keep):
    stride = C // SRC
    bin_index = jnp.arange(F, dtype=jnp.int32)
    lower = jnp.maximum(bin_index - HALF, 0)
    upper = jnp.minimum(bin_index + HALF, F - 1)
    window_count = (upper - lower + 1).astype(jnp.float32)
    whitened = []
    for day_index in range(DAYS):
        spectrum = jnp.fft.rfft(noise[day_index].astype(jnp.float32), axis=-1)[..., LOW:LOW + F]
        real_part = jnp.real(spectrum).astype(jnp.float32)
        imag_part = jnp.imag(spectrum).astype(jnp.float32)
        magnitude = jnp.sqrt(real_part * real_part + imag_part * imag_part)
        cumulative = jnp.concatenate([jnp.zeros_like(magnitude[..., :1]), jnp.cumsum(magnitude, axis=-1)], axis=-1)
        levels = (jnp.take(cumulative, upper + 1, axis=-1) - jnp.take(cumulative, lower, axis=-1)) / window_count + 1e-06
        keep_float = keep[day_index].astype(jnp.float32)[..., None]
        whitened.append(jnp.stack([(keep_float * real_part / levels).astype(jnp.bfloat16), (keep_float * imag_part / levels).astype(jnp.bfloat16)]))
    whitened = jnp.stack(whitened, axis=1)
    sources = whitened[:, :, :, ::stride, :]
    keep_all = keep.astype(jnp.float32)
    pair_floor = jnp.maximum(jnp.einsum('dws,dwc->dsc', keep_all[:, :, ::stride], keep_all), 1.0)
    lag_index = jnp.arange(LAGS, dtype=jnp.int32) - MAXLAG
    lag_phase = jnp.mod((LOW + bin_index)[None, :] * lag_index[:, None], TLEN)
    lag_angle = 2.0 * math.pi / TLEN * lag_phase.astype(jnp.float32)
    cosine = jnp.cos(lag_angle).astype(jnp.bfloat16)
    sine = jnp.sin(lag_angle).astype(jnp.bfloat16)
    block = 8

    def add_block(index, stacked):
        first = (index * block).astype(jnp.int32)
        channel_part = lax.dynamic_slice_in_dim(whitened, first, block, 4).astype(jnp.float32)
        source_part = lax.dynamic_slice_in_dim(sources, first, block, 4).astype(jnp.float32)
        cross_real = jnp.einsum('dwsf,dwcf->dfsc', source_part[0], channel_part[0]) + jnp.einsum('dwsf,dwcf->dfsc', source_part[1], channel_part[1])
        cross_imag = jnp.einsum('dwsf,dwcf->dfsc', source_part[0], channel_part[1]) - jnp.einsum('dwsf,dwcf->dfsc', source_part[1], channel_part[0])
        normed_real = lax.optimization_barrier((cross_real / pair_floor[:, None]).astype(jnp.bfloat16))
        normed_imag = lax.optimization_barrier((cross_imag / pair_floor[:, None]).astype(jnp.bfloat16))
        day_real = lax.optimization_barrier(jnp.sum(normed_real.astype(jnp.float32), axis=0))
        day_imag = lax.optimization_barrier(jnp.sum(normed_imag.astype(jnp.float32), axis=0))
        cosine_part = lax.dynamic_slice_in_dim(cosine, first, block, 1).astype(jnp.float32)
        sine_part = lax.dynamic_slice_in_dim(sine, first, block, 1).astype(jnp.float32)
        return stacked + jnp.einsum('lf,fsc->slc', cosine_part, day_real) - jnp.einsum('lf,fsc->slc', sine_part, day_imag)
    stacked = lax.fori_loop(0, F // block, add_block, jnp.zeros((SRC, LAGS, C), jnp.float32))
    return stacked * (1.0 / math.sqrt(F))
```

```python
import functools
import math

import jax
import jax.numpy as jnp
import ml_dtypes
import numpy as np
from jax import lax
from jax.experimental import pallas as pl
from jax.experimental.pallas import tpu as pltpu
from jax.sharding import PartitionSpec as P

MESH = pl.DeviceIdType.MESH
BF16 = jnp.bfloat16
F32 = jnp.float32

F = 256
LOW = 60
HALF = 64
MAXLAG = 25
LAGS = 2 * MAXLAG + 1
TLEN = 1500
CH = 256
WIN = 8
GROUP = 4
ROWS = 208
TOP = 112
KROWS = 2 * F + 16
FIRST = 272
SLANES = F + 128
H = 1
CP = CH // H


def tables():
    k = np.arange(F)
    t = np.arange(TLEN)
    angle = 2.0 * np.pi / TLEN * ((LOW + k)[:, None] * t[None, :] % TLEN)
    twiddle = np.concatenate([np.cos(angle), -np.sin(angle)], axis=0).astype(np.float32)
    high = twiddle.astype(ml_dtypes.bfloat16)
    rest = (twiddle - high.astype(np.float32)).astype(ml_dtypes.bfloat16)
    band = (np.abs(k[:, None] - k[None, :]) <= HALF).astype(ml_dtypes.bfloat16)
    lag = np.arange(LAGS) - MAXLAG
    lag_angle = 2.0 * np.pi / TLEN * ((LOW + k)[None, :] * lag[:, None] % TLEN)
    cosine = np.zeros((ROWS, F), np.float32)
    sine = np.zeros((ROWS, F), np.float32)
    cosine[: GROUP * LAGS] = np.repeat(np.cos(lag_angle), GROUP, axis=0)
    sine[: GROUP * LAGS] = np.repeat(np.sin(lag_angle), GROUP, axis=0)
    rep = np.zeros((64, 16), ml_dtypes.bfloat16)
    for g in range(2):
        for part in range(2):
            for i in range(16):
                rep[g * 32 + part * 16 + i, part * 8 + g * GROUP + i % GROUP] = 1
    pick = np.zeros((16, CH), ml_dtypes.bfloat16)
    for i in range(16):
        pick[i, (i % 8) * 32] = 1
    return (
        high,
        rest,
        band,
        cosine.astype(ml_dtypes.bfloat16),
        sine.astype(ml_dtypes.bfloat16),
        rep,
        pick,
    )


def kernel(
    noise, keep, high, rest, band, cosine, sine, rep, pick, out,
    wall, sown, sfin, tmat, flags, acc, part, fold_up, fold_down, got_up, got_down,
    w_send, w_recv, s1_send, s1_recv, s2_send, s2_recv, s3_send, s3_recv, d_send, d_recv,
):
    row, col, day = lax.axis_index("row"), lax.axis_index("col"), lax.axis_index("day")
    z, x = row // 4, row % 4
    y, core = col // 2, col % 2
    side = x % 2
    holder = core == x // 2
    collector = jnp.logical_and(holder, y == z)
    upper = ((y + 1) % 4) * 2 + core
    lower = ((y + 3) % 4) * 2 + core
    far = ((y + 2) % 4) * 2 + core
    sibling = y * 2 + 1 - core

    def device(r=row, c=col, d=day):
        return (r, c, d)

    def remote(src, dst, send, recv, target):
        return pltpu.make_async_remote_copy(
            src_ref=src, dst_ref=dst, send_sem=send, recv_sem=recv,
            device_id=target, device_id_type=MESH,
        )

    barrier = pltpu.get_barrier_semaphore()
    partners = [device(c=(col + i) % 8) for i in range(1, 8)]
    partners += [device(r=z * 4 + (x + i) % 4) for i in range(1, 4)]
    partners += [device(r=((z + i) % 4) * 4 + x) for i in range(1, 4)]
    partners += [device(d=(day + i) % 4) for i in (1, 3)]
    for partner in partners:
        pl.semaphore_signal(barrier, inc=1, device_id=partner, device_id_type=MESH)

    spectrum = jnp.dot(high[...], noise[...], preferred_element_type=F32)
    spectrum += jnp.dot(rest[...], noise[...], preferred_element_type=F32)
    real, imag = spectrum[:F], spectrum[F:]
    magnitude = jnp.sqrt(real * real + imag * imag)
    total = jnp.dot(band[...], magnitude.astype(BF16), preferred_element_type=F32)
    bins = lax.broadcasted_iota(jnp.int32, (F, CH), 0)
    count = jnp.minimum(bins + HALF, F - 1) - jnp.maximum(bins - HALF, 0) + 1
    levels = total / count.astype(F32) + 1e-6
    keep_row = keep[...].astype(F32)
    scale = keep_row / levels
    white = jnp.concatenate([real * scale, imag * scale], axis=0).astype(BF16)
    keep_rows = jnp.broadcast_to(keep_row, (16, CH)).astype(BF16)
    for h in range(H):
        cut = slice(h * CP, (h + 1) * CP)
        wall[h, col, 0 : 2 * F, :] = white[:, cut]
        wall[h, col, 2 * F : KROWS, :] = keep_rows[:, cut]

    picked = lax.dot_general(
        pick[...], white, (((1,), (1,)), ((), ())), preferred_element_type=F32
    )
    lower_half = lax.broadcasted_iota(jnp.int32, (16, F), 0) < 8
    mixed = jnp.where(lower_half, picked[:, :F], picked[:, F:])
    flag = jnp.sum(pick[...].astype(F32) * keep_row, axis=1, keepdims=True)
    message = jnp.concatenate([mixed, jnp.broadcast_to(flag, (16, 128))], axis=1).astype(BF16)

    pl.semaphore_wait(barrier, len(partners))

    @pl.when(collector)
    def _():
        sfin[side, col] = message

    @pl.when(jnp.logical_not(collector))
    def _():
        sown[...] = message
        remote(
            sown, sfin.at[side, col], s1_send, s1_recv.at[col], device(c=row // 2)
        ).start()

    def block(h, w, rows=None):
        if rows is None:
            return wall.at[h, w]
        return wall.at[h, w, pl.ds(rows[0], rows[1]), :]

    top, bottom = (0, FIRST), (FIRST, KROWS - FIRST)

    def w_copy(h, index):
        w, rows, target = [
            (col, None, upper),
            (col, None, lower),
            (col, None, sibling),
            (lower, None, sibling),
            (upper, None, sibling),
            (lower, top, upper),
            (upper, bottom, lower),
            (far, top, sibling),
            (far, bottom, sibling),
        ][index]
        ref = block(h, w, rows)
        return remote(ref, ref, w_send.at[h, index], w_recv.at[h, index], device(c=target))

    other = 1 - core

    def w_arrival(h, index):
        w, rows = [
            (lower, None),
            (upper, None),
            (sibling, None),
            (((y + 3) % 4) * 2 + other, None),
            (((y + 1) % 4) * 2 + other, None),
            (far, top),
            (far, bottom),
            (((y + 2) % 4) * 2 + other, top),
            (((y + 2) % 4) * 2 + other, bottom),
        ][index]
        ref = block(h, w, rows)
        remote(ref, ref, w_send.at[h, index], w_recv.at[h, index], device(c=sibling)).wait_recv()

    for h in range(H):
        for index in (0, 1, 2):
            w_copy(h, index).start()

    def s2_copy(i):
        ref = sfin.at[side]
        return remote(ref, ref, s2_send.at[i - 1], s2_recv, device(r=((z + i) % 4) * 4 + x))

    def s3_copy(i):
        ref = sfin.at[side]
        return remote(
            ref, ref, s3_send.at[i - 1], s3_recv.at[side], device(r=z * 4 + (x + i) % 4)
        )

    @pl.when(collector)
    def _():
        for i in range(1, 8):
            w = (col + i) % 8
            remote(
                sown, sfin.at[side, w], s1_send, s1_recv.at[w], device(c=(col + i) % 8)
            ).wait_recv()
        for i in (1, 2, 3):
            s2_copy(i).start()

    @pl.when(jnp.logical_and(holder, jnp.logical_not(collector)))
    def _():
        s2_copy(1).wait_recv()

    @pl.when(holder)
    def _():
        for i in (1, 2, 3):
            s3_copy(i).start()

    for h in range(H):
        w_arrival(h, 0)
        w_copy(h, 3).start()
        w_copy(h, 5).start()
        w_arrival(h, 1)
        w_copy(h, 4).start()
        w_copy(h, 6).start()

    for e in range(2):
        @pl.when(jnp.logical_not(jnp.logical_and(holder, side == e)))
        def _():
            ref = sfin.at[e]
            remote(ref, ref, s3_send.at[0], s3_recv.at[e], device(r=z * 4 + (x + 1) % 4)).wait_recv()

        def make(w, carry):
            spread = jnp.dot(rep[...], sfin[e, w], preferred_element_type=F32)
            for g in range(2):
                base = 32 * g
                s_real = spread[base : base + 16, :F].astype(BF16)[None]
                s_imag = spread[base + 16 : base + 32, :F].astype(BF16)[None]
                flags[w, 2 * e + g] = spread[base : base + 16, F:]
                cos3 = cosine[...].reshape(ROWS // 16, 16, F)
                sin3 = sine[...].reshape(ROWS // 16, 16, F)
                t_real = s_real * cos3 + s_imag * sin3
                t_imag = s_imag * cos3 - s_real * sin3
                tmat[w, 2 * e + g, :, :F] = t_real.reshape(ROWS, F)
                tmat[w, 2 * e + g, :, F:] = t_imag.reshape(ROWS, F)
            return carry

        lax.fori_loop(0, WIN, make, 0)

    for h in range(H):
        def add(w, first=False):
            def body(d, carry):
                value = jnp.dot(
                    tmat[w, d], wall[h, w, 0 : 2 * F, :], preferred_element_type=F32
                )
                acc[d] = value if first else acc[d] + value
                return carry
            lax.fori_loop(0, 4, body, 0)

        add(col, True)
        w_arrival(h, 2)
        add(sibling)
        add(lower)
        add(upper)
        w_arrival(h, 3)
        add(((y + 3) % 4) * 2 + other)
        w_arrival(h, 4)
        add(((y + 1) % 4) * 2 + other)
        w_arrival(h, 5)
        w_copy(h, 7).start()
        w_arrival(h, 6)
        w_copy(h, 8).start()
        add(far)
        w_arrival(h, 7)
        w_arrival(h, 8)
        add(((y + 2) % 4) * 2 + other)

        def partial(d):
            pairs = jnp.zeros((16, CP), F32)
            for w in range(WIN):
                kept = wall[h, w, 2 * F : KROWS, :].astype(F32)
                flag = flags[w, d]
                if CP == CH:
                    flag = jnp.concatenate([flag, flag], axis=1)
                pairs += flag * kept
            inverse = (1.0 / math.sqrt(F)) / jnp.maximum(pairs, 1.0)
            return (acc[d].reshape(ROWS // 16, 16, CP) * inverse[None]).reshape(ROWS, CP)

        def d_copy(index):
            src, dst, target = [
                (part.at[h, 0, pl.ds(0, TOP), :], fold_up.at[h], 1),
                (part.at[h, 0, pl.ds(TOP, ROWS - TOP), :], fold_down.at[h], 3),
                (part.at[h, 1], got_up.at[h], 1),
                (part.at[h, 2], got_down.at[h], 3),
            ][index]
            return remote(
                src, dst, d_send.at[h, index], d_recv.at[h, index], device(d=(day + target) % 4)
            )

        part[h, 0] = partial((day + 2) % 4).astype(BF16)
        d_copy(0).start()
        d_copy(1).start()
        plus = partial((day + 1) % 4)
        minus = partial((day + 3) % 4)
        own = partial(day)
        d_copy(0).wait_recv()
        part[h, 1, 0:TOP, :] = (plus[:TOP] + fold_up[h].astype(F32)).astype(BF16)
        part[h, 1, TOP:, :] = plus[TOP:].astype(BF16)
        d_copy(2).start()
        d_copy(1).wait_recv()
        part[h, 2, 0:TOP, :] = minus[:TOP].astype(BF16)
        part[h, 2, TOP:, :] = (minus[TOP:] + fold_down[h].astype(F32)).astype(BF16)
        d_copy(3).start()
        d_copy(2).wait_recv()
        d_copy(3).wait_recv()
        result = own + got_up[h].astype(F32) + got_down[h].astype(F32)
        out[:, h * CP : (h + 1) * CP] = result

    @pl.when(jnp.logical_not(collector))
    def _():
        remote(
            sown, sfin.at[side, col], s1_send, s1_recv.at[col], device(c=row // 2)
        ).wait_send()

    @pl.when(collector)
    def _():
        for i in (1, 2, 3):
            s2_copy(i).wait_send()

    @pl.when(holder)
    def _():
        for i in (1, 2, 3):
            s3_copy(i).wait_send()

    for h in range(H):
        for index in range(9):
            w_copy(h, index).wait_send()
        for index in range(4):
            d_copy(index).wait_send()


def shards(noise, keep):
    samples = noise[0, 0].T
    consts = tables()
    dma = pltpu.SemaphoreType.DMA
    result = pl.pallas_call(
        kernel,
        out_shape=jax.ShapeDtypeStruct((ROWS, CH), F32),
        in_specs=[pl.BlockSpec(memory_space=pltpu.VMEM)] * (2 + len(consts)),
        out_specs=pl.BlockSpec(memory_space=pltpu.VMEM),
        scratch_shapes=[
            pltpu.VMEM((H, WIN, KROWS, CP), BF16),
            pltpu.VMEM((16, SLANES), BF16),
            pltpu.VMEM((2, WIN, 16, SLANES), BF16),
            pltpu.VMEM((WIN, 4, ROWS, 2 * F), BF16),
            pltpu.VMEM((WIN, 4, 16, 128), F32),
            pltpu.VMEM((4, ROWS, CP), F32),
            pltpu.VMEM((H, 3, ROWS, CP), BF16),
            pltpu.VMEM((H, TOP, CP), BF16),
            pltpu.VMEM((H, ROWS - TOP, CP), BF16),
            pltpu.VMEM((H, ROWS, CP), BF16),
            pltpu.VMEM((H, ROWS, CP), BF16),
            dma((H, 9)),
            dma((H, 9)),
            dma,
            dma((8,)),
            dma((3,)),
            dma,
            dma((3,)),
            dma((2,)),
            dma((H, 4)),
            dma((H, 4)),
        ],
        compiler_params=pltpu.CompilerParams(
            collective_id=0, has_side_effects=True, vmem_limit_bytes=48 * 1024 * 1024
        ),
    )(samples, keep[0], *[jnp.asarray(c) for c in consts])
    return result[: GROUP * LAGS].reshape(LAGS, GROUP, CH).transpose(1, 0, 2)


def solution(mesh):
    in_specs = (P("day", "col", "row", None), P("day", "col", "row"))
    out_specs = P(("col", "day"), None, "row")
    return jax.shard_map(shards, mesh=mesh, in_specs=in_specs, out_specs=out_specs, check_vma=False)
```

```python
import functools
import math

import jax
import jax.numpy as jnp
import ml_dtypes
import numpy as np
from jax import lax
from jax.experimental import pallas as pl
from jax.experimental.pallas import tpu as pltpu
from jax.sharding import PartitionSpec as P

MESH = pl.DeviceIdType.MESH
BF16 = jnp.bfloat16
F32 = jnp.float32

F = 256
LOW = 60
HALF = 64
MAXLAG = 25
LAGS = 2 * MAXLAG + 1
TLEN = 1500
CH = 256
WIN = 8
GROUP = 4
ROWS = 208
TOP = 112
SLANES = F + 128
H = 2
CP = CH // H


def tables():
    k = np.arange(F)
    t = np.arange(TLEN)
    angle = 2.0 * np.pi / TLEN * ((LOW + k)[:, None] * t[None, :] % TLEN)
    twiddle = np.concatenate([np.cos(angle), -np.sin(angle)], axis=0).astype(np.float32)
    high = twiddle.astype(ml_dtypes.bfloat16)
    rest = (twiddle - high.astype(np.float32)).astype(ml_dtypes.bfloat16)
    band = (np.abs(k[:, None] - k[None, :]) <= HALF).astype(ml_dtypes.bfloat16)
    lag = np.arange(LAGS) - MAXLAG
    lag_angle = 2.0 * np.pi / TLEN * ((LOW + k)[None, :] * lag[:, None] % TLEN)
    cosine = np.zeros((ROWS, F), np.float32)
    sine = np.zeros((ROWS, F), np.float32)
    cosine[: GROUP * LAGS] = np.repeat(np.cos(lag_angle), GROUP, axis=0)
    sine[: GROUP * LAGS] = np.repeat(np.sin(lag_angle), GROUP, axis=0)
    rep = np.zeros((64, 16), ml_dtypes.bfloat16)
    for g in range(2):
        for part in range(2):
            for i in range(16):
                rep[g * 32 + part * 16 + i, part * 8 + g * GROUP + i % GROUP] = 1
    pick = np.zeros((16, CH), ml_dtypes.bfloat16)
    for i in range(16):
        pick[i, (i % 8) * 32] = 1
    return (
        high,
        rest,
        band,
        cosine.astype(ml_dtypes.bfloat16),
        sine.astype(ml_dtypes.bfloat16),
        rep,
        pick,
    )


def kernel(
    noise_hbm, keep_hbm, high_hbm, rest_hbm, band_hbm, cosine_hbm, sine_hbm, rep_hbm, pick_hbm, out,
    noise, keep, high, rest, band, cosine, sine, rep, pick, load,
    wall, kept, marks, sown, held, sfin, spread, tmat, inverse, own, near, part, fold_up, fold_down, got_up, got_down,
    w_send, w_recv, k_send, k_recv, s_send, s_recv, t_send, t_recv, d_send, d_recv,
):
    loads = [
        pltpu.make_async_copy(src, dst, load.at[i])
        for i, (src, dst) in enumerate(
            [
                (noise_hbm, noise),
                (keep_hbm, keep),
                (high_hbm, high),
                (rest_hbm, rest),
                (band_hbm, band),
                (pick_hbm, pick),
                (rep_hbm, rep),
                (cosine_hbm, cosine),
                (sine_hbm, sine),
            ]
        )
    ]
    for copy in loads:
        copy.start()

    row, col, day = lax.axis_index("row"), lax.axis_index("col"), lax.axis_index("day")
    z, x = row // 4, row % 4
    y, core = col // 2, col % 2
    side = x % 2
    holder = core == x // 2
    home = jnp.logical_and(holder, y == z)
    away = jnp.logical_not(home)

    def column(step, flip=0):
        return ((y + step) % 4) * 2 + (core + flip) % 2

    upper, lower, far, sibling = column(1), column(3), column(2), column(0, 1)

    def device(r=row, c=col, d=day):
        return (r, c, d)

    def remote(src, dst, send, recv, target):
        return pltpu.make_async_remote_copy(
            src_ref=src, dst_ref=dst, send_sem=send, recv_sem=recv,
            device_id=target, device_id_type=MESH,
        )

    barrier = pltpu.get_barrier_semaphore()

    def greet(target):
        pl.semaphore_signal(barrier, inc=1, device_id=target, device_id_type=MESH)

    for i in range(1, 8):
        greet(device(c=(col + i) % 8))
    for i in (1, 3):
        greet(device(d=(day + i) % 4))
    @pl.when(holder)
    def _():
        for i in range(8):
            if i:
                greet(device(r=4 * y + x, c=(col + i) % 8))
            else:

                @pl.when(away)
                def _():
                    greet(device(r=4 * y + x))

    for e in range(2):

        @pl.when(x != 2 * core + e)
        def _():
            greet(device(r=4 * z + 2 * core + e))

    for copy in loads[:3]:
        copy.wait()
    spectrum = jnp.dot(high[...], noise[...], preferred_element_type=F32)
    loads[3].wait()
    spectrum += jnp.dot(rest[...], noise[...], preferred_element_type=F32)
    real, imag = spectrum[:F], spectrum[F:]
    magnitude = jnp.sqrt(real * real + imag * imag)
    loads[4].wait()
    total = jnp.dot(band[...], magnitude.astype(BF16), preferred_element_type=F32)
    bins = lax.broadcasted_iota(jnp.int32, (F, CH), 0)
    count = jnp.minimum(bins + HALF, F - 1) - jnp.maximum(bins - HALF, 0) + 1
    levels = total / count.astype(F32) + 1e-6
    keep_row = keep[...].astype(F32)
    scale = keep_row / levels
    white = jnp.concatenate([real * scale, imag * scale], axis=0).astype(BF16)
    for h in range(H):
        wall[h, col] = white[:, h * CP : (h + 1) * CP]
    kept[col] = jnp.concatenate(
        [jnp.broadcast_to(keep_row[:, :128], (8, 128)), jnp.broadcast_to(keep_row[:, 128:], (8, 128))]
    ).astype(BF16)
    marks[...] = jnp.zeros_like(marks)

    loads[5].wait()
    picked = lax.dot_general(
        pick[...], white, (((1,), (1,)), ((), ())), preferred_element_type=F32
    )
    lower_half = lax.broadcasted_iota(jnp.int32, (16, F), 0) < 8
    mixed = jnp.where(lower_half, picked[:, :F], picked[:, F:])
    flag = jnp.sum(pick[...].astype(F32) * keep_row, axis=1, keepdims=True)
    message = jnp.concatenate([mixed, jnp.broadcast_to(flag, (16, 128))], axis=1).astype(BF16)
    sown[...] = message

    @pl.when(home)
    def _():
        held[col] = message

    pl.semaphore_wait(barrier, 7 + 2 + 3 + away.astype(jnp.int32) + 3 * holder.astype(jnp.int32))

    def s_copy(k):
        target = device(r=((z + k) % 4) * 4 + x, c=row // 2)
        return remote(sown, held.at[col], s_send.at[k], s_recv.at[col], target)

    def s_each(method):
        for k in (1, 2, 3):
            getattr(s_copy(k), method)()

        @pl.when(away)
        def _():
            getattr(s_copy(0), method)()

    s_each("start")

    def t_copy(i):
        ref = sfin.at[side]
        target = device(r=z * 4 + (x + i) % 4)
        return remote(ref, ref, t_send.at[i - 1], t_recv.at[side], target)

    def s_forward():
        @pl.when(holder)
        def _():
            for w in range(WIN):

                @pl.when(jnp.logical_not(home & (col == w)))
                def _():
                    remote(
                        sown, held.at[w], s_send.at[0], s_recv.at[w], device(c=sibling)
                    ).wait_recv()

            lane = lax.broadcasted_iota(jnp.int32, (16, 128), 1)
            mark = jnp.zeros((16, 128), F32)
            for w in range(WIN):
                sfin[side, w] = held[w, :, 0:F]
                mark = jnp.where(lane == w, held[w, :, F:].astype(F32), mark)
            sfin[side, WIN] = jnp.concatenate([mark, mark], axis=1).astype(BF16)

    def s_spread(e):
        @pl.when(holder & (side == e))
        def _():
            for i in (1, 2, 3):
                t_copy(i).start()

    def s_arrival(e):
        @pl.when(jnp.logical_not(holder & (side == e)))
        def _():
            ref = sfin.at[e]
            remote(ref, ref, t_send.at[0], t_recv.at[e], device(c=sibling)).wait_recv()

    top, bottom = (0, F), (F, F)

    def block(h, w, rows):
        if rows is None:
            return wall.at[h, w]
        return wall.at[h, w, pl.ds(rows[0], rows[1]), :]

    routes = [
        (col, top, upper, lower),
        (col, bottom, lower, upper),
        (col, bottom, upper, lower),
        (col, top, lower, upper),
        (col, None, sibling, sibling),
        (lower, top, upper, far),
        (upper, bottom, lower, far),
        (lower, None, sibling, column(3, 1)),
        (upper, None, sibling, column(1, 1)),
        (far, top, sibling, column(2, 1)),
        (far, bottom, sibling, column(2, 1)),
    ]

    def w_copy(h, index):
        w, rows, target, _ = routes[index]
        ref = block(h, w, rows)
        return remote(ref, ref, w_send.at[h, index], w_recv.at[h, index], device(c=target))

    def w_arrival(h, *indices):
        for index in indices:
            _, rows, _, w = routes[index]
            ref = block(h, w, rows)
            remote(
                ref, ref, w_send.at[h, index], w_recv.at[h, index], device(c=sibling)
            ).wait_recv()

    def w_start(h, *indices):
        for index in indices:
            w_copy(h, index).start()

    def k_copy(i):
        ref = kept.at[col]
        return remote(ref, ref, k_send.at[i - 1], k_recv.at[i - 1], device(c=(col + i) % 8))

    def first_hop(h):
        w_start(h, 0, 1)

    def second_hop(h):
        w_arrival(h, 0)
        w_start(h, 5)
        w_arrival(h, 1)
        w_start(h, 6, 2, 3, 4)

    def third_hop(h):
        w_arrival(h, 2)
        w_start(h, 7)
        w_arrival(h, 3)
        w_start(h, 8)
        w_arrival(h, 5)
        w_start(h, 9)
        w_arrival(h, 6)
        w_start(h, 10)

    def last_hop(h):
        w_arrival(h, 4, 7, 8, 9, 10)

    def spread_sources(e):
        def body(w, carry):
            rows = jnp.dot(rep[...], sfin[e, w], preferred_element_type=F32)
            spread[e, w] = rows.astype(BF16)
            return carry

        lax.fori_loop(0, WIN, body, 0, unroll=4)

    def count_pairs(e):
        rows = jnp.dot(rep[...], sfin[e, WIN, :, 0:128], preferred_element_type=F32)
        pairs = jnp.dot(rows.astype(BF16), marks[...], preferred_element_type=F32)
        for g in range(2):
            floor = jnp.maximum(pairs[32 * g : 32 * g + 16], 1.0)
            inverse[2 * e + g] = (1.0 / math.sqrt(F)) / floor

    def make(d):
        e, g = d // 2, d % 2
        real_rows = pl.ds(pl.multiple_of(32 * g, 32), 16)
        imag_rows = pl.ds(pl.multiple_of(32 * g + 16, 16), 16)

        def body(w, carry):
            s_real = spread[e, w, real_rows, :]
            s_imag = spread[e, w, imag_rows, :]
            at = pl.multiple_of(w * 2 * F, 2 * F)
            for t in range(ROWS // 16):
                rows = slice(16 * t, 16 * t + 16)
                cos_rows, sin_rows = cosine[rows, :], sine[rows, :]
                tmat[d, rows, pl.ds(at, F)] = s_real * cos_rows + s_imag * sin_rows
                tmat[d, rows, pl.ds(at + F, F)] = s_imag * cos_rows - s_real * sin_rows
            return carry

        lax.fori_loop(0, WIN, body, 0)

    def partial(h, d):
        value = jnp.dot(
            tmat[d], wall[h].reshape(WIN * 2 * F, CP), preferred_element_type=F32
        )
        factor = inverse[d, :, h * CP : (h + 1) * CP]
        return (value.reshape(ROWS // 16, 16, CP) * factor[None]).reshape(ROWS, CP)

    up, down, away_day = (day + 1) % 4, (day + 3) % 4, (day + 2) % 4
    head, tail = pl.ds(0, TOP), pl.ds(TOP, ROWS - TOP)

    def d_copy(h, index):
        src, dst, target = [
            (part.at[h, 0, head, :], fold_up.at[h], up),
            (part.at[h, 0, tail, :], fold_down.at[h], down),
            (part.at[h, 1, tail, :], got_up.at[h, tail, :], up),
            (part.at[h, 2, head, :], got_down.at[h, head, :], down),
            (part.at[h, 1, head, :], got_up.at[h, head, :], up),
            (part.at[h, 2, tail, :], got_down.at[h, tail, :], down),
        ][index]
        return remote(src, dst, d_send.at[h, index], d_recv.at[h, index], device(d=target))

    def send_far(h):
        part[h, 0] = partial(h, away_day).astype(BF16)
        d_copy(h, 0).start()
        d_copy(h, 1).start()

    def send_near(h):
        plus = partial(h, up)
        near[h, 0] = plus
        part[h, 1, TOP:, :] = plus[TOP:].astype(BF16)
        minus = partial(h, down)
        near[h, 1] = minus
        part[h, 2, 0:TOP, :] = minus[:TOP].astype(BF16)
        d_copy(h, 0).wait_send()
        d_copy(h, 2).start()
        d_copy(h, 1).wait_send()
        d_copy(h, 3).start()

    def send_folded(h):
        d_copy(h, 0).wait_recv()
        part[h, 1, 0:TOP, :] = (near[h, 0, 0:TOP, :] + fold_up[h].astype(F32)).astype(BF16)
        d_copy(h, 4).start()
        d_copy(h, 1).wait_recv()
        part[h, 2, TOP:, :] = (near[h, 1, TOP:, :] + fold_down[h].astype(F32)).astype(BF16)
        d_copy(h, 5).start()

    def finish(h):
        for index in (2, 3, 4, 5):
            d_copy(h, index).wait_recv()
        result = own[h] + got_up[h].astype(F32) + got_down[h].astype(F32)
        out[:, h * CP : (h + 1) * CP] = result

    def k_arrival():
        for i in range(1, 8):
            ref = kept.at[(col + 8 - i) % 8]
            remote(ref, ref, k_send.at[i - 1], k_recv.at[i - 1], device(c=sibling)).wait_recv()
        rows = [
            jnp.concatenate([kept[w, 0:1, :], kept[w, 8:9, :]], axis=1).astype(F32)
            for w in range(WIN)
        ]
        marks[0:16, :] = jnp.concatenate(rows + [jnp.zeros((8, CH), F32)]).astype(BF16)

    first_side = away_day // 2
    first_hop(0)
    for i in range(1, 8):
        k_copy(i).start()
    s_forward()
    s_spread(first_side)
    second_hop(0)
    s_spread(1 - first_side)
    for copy in loads[6:]:
        copy.wait()
    s_arrival(first_side)
    first_hop(1)
    spread_sources(first_side)
    k_arrival()
    count_pairs(first_side)
    make(away_day)
    third_hop(0)
    last_hop(0)
    send_far(0)
    second_hop(1)
    s_arrival(1 - first_side)
    spread_sources(1 - first_side)
    count_pairs(1 - first_side)
    make(up)
    make(down)
    send_near(0)
    third_hop(1)
    send_folded(0)
    last_hop(1)
    send_far(1)
    make(day)
    send_near(1)
    own[0] = partial(0, day)
    send_folded(1)
    own[1] = partial(1, day)
    finish(0)
    finish(1)

    s_each("wait_send")

    @pl.when(holder)
    def _():
        for i in (1, 2, 3):
            t_copy(i).wait_send()

    for i in range(1, 8):
        k_copy(i).wait_send()
    for h in range(H):
        for index in range(11):
            w_copy(h, index).wait_send()
        for index in (2, 3, 4, 5):
            d_copy(h, index).wait_send()


def shards(noise, keep):
    samples = noise[0, 0].T
    consts = tables()
    dma = pltpu.SemaphoreType.DMA
    result = pl.pallas_call(
        kernel,
        out_shape=jax.ShapeDtypeStruct((ROWS, CH), F32),
        in_specs=[
            pl.BlockSpec(memory_space=pltpu.HBM)
            for i in range(2 + len(consts))
        ],
        out_specs=pl.BlockSpec(memory_space=pltpu.VMEM),
        scratch_shapes=[
            pltpu.VMEM(samples.shape, BF16),
            pltpu.VMEM((1, CH), jnp.int32),
            *[pltpu.VMEM(c.shape, BF16) for c in consts],
            dma((2 + len(consts),)),
            pltpu.VMEM((H, WIN, 2 * F, CP), BF16),
            pltpu.VMEM((WIN, 16, 128), BF16),
            pltpu.VMEM((128, CH), BF16),
            pltpu.VMEM((16, SLANES), BF16),
            pltpu.VMEM((WIN, 16, SLANES), BF16),
            pltpu.VMEM((2, WIN + 1, 16, F), BF16),
            pltpu.VMEM((2, WIN, 64, F), BF16),
            pltpu.VMEM((4, ROWS, WIN * 2 * F), BF16),
            pltpu.VMEM((4, 16, CH), F32),
            pltpu.VMEM((H, ROWS, CP), F32),
            pltpu.VMEM((H, 2, ROWS, CP), F32),
            pltpu.VMEM((H, 3, ROWS, CP), BF16),
            pltpu.VMEM((H, TOP, CP), BF16),
            pltpu.VMEM((H, ROWS - TOP, CP), BF16),
            pltpu.VMEM((H, ROWS, CP), BF16),
            pltpu.VMEM((H, ROWS, CP), BF16),
            dma((H, 11)),
            dma((H, 11)),
            dma((7,)),
            dma((7,)),
            dma((4,)),
            dma((WIN,)),
            dma((3,)),
            dma((2,)),
            dma((H, 6)),
            dma((H, 6)),
        ],
        compiler_params=pltpu.CompilerParams(
            collective_id=0, has_side_effects=True, vmem_limit_bytes=60 * 1024 * 1024
        ),
    )(samples, keep[0], *[jnp.asarray(c) for c in consts])
    return result[: GROUP * LAGS].reshape(LAGS, GROUP, CH).transpose(1, 0, 2)


def solution(mesh):
    in_specs = (P("day", "col", "row", None), P("day", "col", "row"))
    out_specs = P(("col", "day"), None, "row")
    return jax.shard_map(shards, mesh=mesh, in_specs=in_specs, out_specs=out_specs, check_vma=False)
```

```python
import functools
import math

import jax
import jax.numpy as jnp
import ml_dtypes
import numpy as np
from jax import lax
from jax.experimental import pallas as pl
from jax.experimental.pallas import tpu as pltpu
from jax.sharding import PartitionSpec as P

MESH = pl.DeviceIdType.MESH
BF16 = jnp.bfloat16
F32 = jnp.float32

F = 256
LOW = 60
HALF = 64
MAXLAG = 25
LAGS = 2 * MAXLAG + 1
TLEN = 1500
CH = 256
WIN = 8
GROUP = 4
HALFRANK = 16
RANK = 2 * HALFRANK
ROWS = GROUP * RANK
TOP = ROWS // 2
OUT = 208
SLANES = F + 128
H = 1
CP = CH // H


def tables():
    k = np.arange(F)
    t = np.arange(TLEN)
    angle = 2.0 * np.pi / TLEN * ((LOW + k)[:, None] * t[None, :] % TLEN)
    twiddle = np.concatenate([np.cos(angle), -np.sin(angle)], axis=0).astype(np.float32)
    high = twiddle.astype(ml_dtypes.bfloat16)
    rest = (twiddle - high.astype(np.float32)).astype(ml_dtypes.bfloat16)
    band = (np.abs(k[:, None] - k[None, :]) <= HALF).astype(ml_dtypes.bfloat16)
    lag = np.arange(LAGS) - MAXLAG
    lag_angle = 2.0 * np.pi / TLEN * ((LOW + k)[None, :] * lag[:, None] % TLEN)
    back, basis = [], []
    for part in (np.cos(lag_angle), -np.sin(lag_angle)):
        left, size, right = np.linalg.svd(part, full_matrices=False)
        left, size, right = left[:, :HALFRANK], size[:HALFRANK], right[:HALFRANK]
        back.append(left * size / 16.0)
        basis.append(right * 16.0)
    basis = np.repeat(np.concatenate(basis), GROUP, axis=0).astype(ml_dtypes.bfloat16)
    synth = np.zeros((OUT, ROWS), np.float32)
    synth[: GROUP * LAGS] = np.kron(np.concatenate(back, axis=1), np.eye(GROUP))
    synth_high = synth.astype(ml_dtypes.bfloat16)
    synth_rest = (synth - synth_high.astype(np.float32)).astype(ml_dtypes.bfloat16)
    synth = np.concatenate([synth_high, synth_high, synth_rest], axis=1)
    rep = np.zeros((64, 16), ml_dtypes.bfloat16)
    for g in range(2):
        for part in range(2):
            for i in range(16):
                rep[g * 32 + part * 16 + i, part * 8 + g * GROUP + i % GROUP] = 1
    pick = np.zeros((16, CH), ml_dtypes.bfloat16)
    for i in range(16):
        pick[i, (i % 8) * 32] = 1
    return (
        high,
        rest,
        band,
        basis,
        synth,
        rep,
        pick,
    )


def kernel(
    noise_hbm, keep_hbm, high_hbm, rest_hbm, band_hbm, basis_hbm, synth_hbm, rep_hbm, pick_hbm, out,
    noise, keep, high, rest, band, basis, synth, rep, pick, load,
    wall, kept, marks, sown, held, sfin, spread, tmat, inverse, own, near, part, fold_up, fold_down, got_up, got_down,
    w_send, w_recv, k_send, k_recv, s_send, s_recv, t_send, t_recv, d_send, d_recv,
):
    loads = [
        pltpu.make_async_copy(src, dst, load.at[i])
        for i, (src, dst) in enumerate(
            [
                (noise_hbm, noise),
                (keep_hbm, keep),
                (high_hbm, high),
                (rest_hbm, rest),
                (band_hbm, band),
                (pick_hbm, pick),
                (rep_hbm, rep),
                (basis_hbm, basis),
                (synth_hbm, synth),
            ]
        )
    ]
    for copy in loads:
        copy.start()

    row, col, day = lax.axis_index("row"), lax.axis_index("col"), lax.axis_index("day")
    z, x = row // 4, row % 4
    y, core = col // 2, col % 2
    side = x % 2
    holder = core == x // 2
    home = jnp.logical_and(holder, y == z)
    away = jnp.logical_not(home)

    def column(step, flip=0):
        return ((y + step) % 4) * 2 + (core + flip) % 2

    upper, lower, far, sibling = column(1), column(3), column(2), column(0, 1)

    def device(r=row, c=col, d=day):
        return (r, c, d)

    def remote(src, dst, send, recv, target):
        return pltpu.make_async_remote_copy(
            src_ref=src, dst_ref=dst, send_sem=send, recv_sem=recv,
            device_id=target, device_id_type=MESH,
        )

    barrier = pltpu.get_barrier_semaphore()

    def greet(target):
        pl.semaphore_signal(barrier, inc=1, device_id=target, device_id_type=MESH)

    for i in range(1, 8):
        greet(device(c=(col + i) % 8))
    for i in (1, 3):
        greet(device(d=(day + i) % 4))
    @pl.when(holder)
    def _():
        for i in range(8):
            if i:
                greet(device(r=4 * y + x, c=(col + i) % 8))
            else:

                @pl.when(away)
                def _():
                    greet(device(r=4 * y + x))

    for e in range(2):

        @pl.when(x != 2 * core + e)
        def _():
            greet(device(r=4 * z + 2 * core + e))

    for copy in loads[:3]:
        copy.wait()
    spectrum = jnp.dot(high[...], noise[...], preferred_element_type=F32)
    loads[3].wait()
    spectrum += jnp.dot(rest[...], noise[...], preferred_element_type=F32)
    loads[4].wait()
    keep_row = keep[...].astype(F32)
    bins = lax.broadcasted_iota(jnp.int32, (F, CP), 0)
    count = jnp.minimum(bins + HALF, F - 1) - jnp.maximum(bins - HALF, 0) + 1
    weight = 1.0 / count.astype(F32)

    def whiten(h):
        cut = slice(h * CP, (h + 1) * CP)
        real, imag = spectrum[:F, cut], spectrum[F:, cut]
        magnitude = jnp.sqrt(real * real + imag * imag)
        total = jnp.dot(band[...], magnitude.astype(BF16), preferred_element_type=F32)
        scale = keep_row[:, cut] / (total * weight + 1e-6)
        white = jnp.concatenate([real * scale, imag * scale], axis=0).astype(BF16)
        wall[h, col] = white
        return white

    white = [whiten(0)]
    def s_copy(k):
        target = device(r=((z + k) % 4) * 4 + x, c=row // 2)
        return remote(sown, held.at[col], s_send.at[k], s_recv.at[col], target)

    def s_each(method):
        for k in (1, 2, 3):
            getattr(s_copy(k), method)()

        @pl.when(away)
        def _():
            getattr(s_copy(0), method)()

    def t_copy(i):
        ref = sfin.at[side]
        target = device(r=z * 4 + (x + i) % 4)
        return remote(ref, ref, t_send.at[i - 1], t_recv.at[side], target)

    def s_forward():
        @pl.when(holder)
        def _():
            for w in range(WIN):

                @pl.when(jnp.logical_not(home & (col == w)))
                def _():
                    remote(
                        sown, held.at[w], s_send.at[0], s_recv.at[w], device(c=sibling)
                    ).wait_recv()

            lane = lax.broadcasted_iota(jnp.int32, (16, 128), 1)
            mark = jnp.zeros((16, 128), F32)
            for w in range(WIN):
                sfin[side, w] = held[w, :, 0:F]
                mark = jnp.where(lane == w, held[w, :, F:].astype(F32), mark)
            sfin[side, WIN] = jnp.concatenate([mark, mark], axis=1).astype(BF16)

    def s_spread(e):
        @pl.when(holder & (side == e))
        def _():
            for i in (2, 1, 3):
                t_copy(i).start()

    def s_arrival(e):
        @pl.when(jnp.logical_not(holder & (side == e)))
        def _():
            ref = sfin.at[e]
            remote(ref, ref, t_send.at[0], t_recv.at[e], device(c=sibling)).wait_recv()

    top, bottom = (0, F), (F, F)

    def block(h, w, rows):
        if rows is None:
            return wall.at[h, w]
        return wall.at[h, w, pl.ds(rows[0], rows[1]), :]

    routes = [
        (col, top, upper, lower),
        (col, bottom, lower, upper),
        (col, bottom, upper, lower),
        (col, top, lower, upper),
        (col, None, sibling, sibling),
        (lower, top, upper, far),
        (upper, bottom, lower, far),
        (lower, None, sibling, column(3, 1)),
        (upper, None, sibling, column(1, 1)),
        (far, top, sibling, column(2, 1)),
        (far, bottom, sibling, column(2, 1)),
    ]

    def w_copy(h, index):
        w, rows, target, _ = routes[index]
        ref = block(h, w, rows)
        return remote(ref, ref, w_send.at[h, index], w_recv.at[h, index], device(c=target))

    def w_arrival(h, *indices):
        for index in indices:
            _, rows, _, w = routes[index]
            ref = block(h, w, rows)
            remote(
                ref, ref, w_send.at[h, index], w_recv.at[h, index], device(c=sibling)
            ).wait_recv()

    def w_start(h, *indices):
        for index in indices:
            w_copy(h, index).start()

    def k_copy(i):
        ref = kept.at[col]
        return remote(ref, ref, k_send.at[i - 1], k_recv.at[i - 1], device(c=(col + i) % 8))

    def first_hop(h):
        w_start(h, 0, 1)

    def rest_hop(h):
        w_start(h, 2, 3, 4)

    def second_hop(h):
        w_arrival(h, 0)
        w_start(h, 5)
        w_arrival(h, 1)
        w_start(h, 6)

    def third_hop(h):
        w_arrival(h, 2)
        w_start(h, 7)
        w_arrival(h, 3)
        w_start(h, 8)

    def fourth_hop(h):
        w_arrival(h, 5)
        w_start(h, 9)
        w_arrival(h, 6)
        w_start(h, 10)

    def last_hop(h):
        w_arrival(h, 4, 7, 8, 9, 10)

    def spread_sources(e):
        def body(w, carry):
            rows = jnp.dot(rep[...], sfin[e, w], preferred_element_type=F32)
            spread[e, w] = rows.astype(BF16)
            return carry

        lax.fori_loop(0, WIN, body, 0, unroll=4)

    def count_pairs(e):
        rows = jnp.dot(rep[...], sfin[e, WIN, :, 0:128], preferred_element_type=F32)
        pairs = jnp.dot(rows.astype(BF16), marks[...], preferred_element_type=F32)
        for g in range(2):
            floor = jnp.maximum(pairs[32 * g : 32 * g + 16], 1.0)
            inverse[2 * e + g] = (1.0 / math.sqrt(F)) / floor

    def make(slot, d):
        e, g = d // 2, d % 2
        real_rows = pl.ds(pl.multiple_of(32 * g, 32), 16)
        imag_rows = pl.ds(pl.multiple_of(32 * g + 16, 16), 16)

        def body(w, carry):
            s_real = spread[e, w, real_rows, :]
            s_imag = spread[e, w, imag_rows, :]
            at = pl.multiple_of(w * 2 * F, 2 * F)
            for t in range(ROWS // 16):
                rows = slice(16 * t, 16 * t + 16)
                table = basis[rows, :]
                first, second = (s_real, s_imag) if 2 * t < ROWS // 16 else (-s_imag, s_real)
                tmat[slot, rows, pl.ds(at, F)] = first * table
                tmat[slot, rows, pl.ds(at + F, F)] = second * table
            return carry

        lax.fori_loop(0, WIN, body, 0)

    def partial(h, slot, d):
        value = jnp.dot(
            tmat[slot], wall[h].reshape(WIN * 2 * F, CP), preferred_element_type=F32
        )
        factor = inverse[d, :, h * CP : (h + 1) * CP]
        return (value.reshape(ROWS // 16, 16, CP) * factor[None]).reshape(ROWS, CP)

    up, down, away_day = (day + 1) % 4, (day + 3) % 4, (day + 2) % 4
    head, tail = pl.ds(0, TOP), pl.ds(TOP, ROWS - TOP)

    def d_copy(h, index):
        src, dst, target = [
            (part.at[h, 0, head, :], fold_up.at[h], up),
            (part.at[h, 0, tail, :], fold_down.at[h], down),
            (part.at[h, 1, tail, :], got_up.at[h, tail, :], up),
            (part.at[h, 2, head, :], got_down.at[h, head, :], down),
            (part.at[h, 1, head, :], got_up.at[h, head, :], up),
            (part.at[h, 2, tail, :], got_down.at[h, tail, :], down),
        ][index]
        return remote(src, dst, d_send.at[h, index], d_recv.at[h, index], device(d=target))

    def send_far(h):
        part[h, 0] = partial(h, 0, away_day).astype(BF16)
        d_copy(h, 0).start()
        d_copy(h, 1).start()

    def compute_near(h):
        plus = partial(h, 1, up)
        near[h, 0] = plus
        part[h, 1, TOP:, :] = plus[TOP:].astype(BF16)
        minus = partial(h, 2, down)
        near[h, 1] = minus
        part[h, 2, 0:TOP, :] = minus[:TOP].astype(BF16)

    def drain_far(h):
        d_copy(h, 0).wait_send()
        d_copy(h, 1).wait_send()

    def send_near(h):
        d_copy(h, 2).start()
        d_copy(h, 3).start()

    def send_folded(h):
        d_copy(h, 0).wait_recv()
        part[h, 1, 0:TOP, :] = (near[h, 0, 0:TOP, :] + fold_up[h].astype(F32)).astype(BF16)
        d_copy(h, 4).start()
        d_copy(h, 1).wait_recv()
        part[h, 2, TOP:, :] = (near[h, 1, TOP:, :] + fold_down[h].astype(F32)).astype(BF16)
        d_copy(h, 5).start()

    def finish(h):
        for index in (2, 3, 4, 5):
            d_copy(h, index).wait_recv()
        result = own[h] + got_up[h].astype(F32) + got_down[h].astype(F32)
        high_part = result.astype(BF16)
        rest_part = (result - high_part.astype(F32)).astype(BF16)
        out[:, h * CP : (h + 1) * CP] = jnp.dot(
            synth[...],
            jnp.concatenate([high_part, rest_part, high_part]),
            preferred_element_type=F32,
        )

    def k_arrival():
        for i in range(1, 8):
            ref = kept.at[(col + 8 - i) % 8]
            remote(ref, ref, k_send.at[i - 1], k_recv.at[i - 1], device(c=sibling)).wait_recv()
        rows = [
            jnp.concatenate([kept[w, 0:1, :], kept[w, 8:9, :]], axis=1).astype(F32)
            for w in range(WIN)
        ]
        marks[0:16, :] = jnp.concatenate(rows + [jnp.zeros((8, CH), F32)]).astype(BF16)

    first_side = away_day // 2
    pl.semaphore_wait(barrier, 7 + 2 + 3 + away.astype(jnp.int32) + 3 * holder.astype(jnp.int32))
    first_hop(0)
    kept[col] = jnp.concatenate(
        [jnp.broadcast_to(keep_row[:, :128], (8, 128)), jnp.broadcast_to(keep_row[:, 128:], (8, 128))]
    ).astype(BF16)
    marks[...] = jnp.zeros_like(marks)

    loads[5].wait()
    picked = jnp.zeros((16, 2 * F), F32)
    for h in range(H):
        picked += lax.dot_general(
            pick[:, h * CP : (h + 1) * CP],
            white[h],
            (((1,), (1,)), ((), ())),
            preferred_element_type=F32,
        )
    lower_half = lax.broadcasted_iota(jnp.int32, (16, F), 0) < 8
    mixed = jnp.where(lower_half, picked[:, :F], picked[:, F:])
    flag = jnp.sum(pick[...].astype(F32) * keep_row, axis=1, keepdims=True)
    message = jnp.concatenate([mixed, jnp.broadcast_to(flag, (16, 128))], axis=1).astype(BF16)
    sown[...] = message

    @pl.when(home)
    def _():
        held[col] = message
    s_each("start")
    rest_hop(0)
    for i in range(1, 8):
        k_copy(i).start()
    second_hop(0)
    s_forward()
    s_spread(first_side)
    s_spread(1 - first_side)
    third_hop(0)
    for copy in loads[6:]:
        copy.wait()
    k_arrival()
    s_arrival(first_side)
    spread_sources(first_side)
    make(0, away_day)
    fourth_hop(0)
    s_arrival(1 - first_side)
    spread_sources(1 - first_side)
    count_pairs(first_side)
    count_pairs(1 - first_side)
    make(1, up)
    make(2, down)
    last_hop(0)
    send_far(0)
    compute_near(0)
    drain_far(0)
    send_near(0)
    make(3, day)
    own[0] = partial(0, 3, day)
    send_folded(0)
    finish(0)

    s_each("wait_send")

    @pl.when(holder)
    def _():
        for i in (1, 2, 3):
            t_copy(i).wait_send()

    for i in range(1, 8):
        k_copy(i).wait_send()
    for h in range(H):
        for index in range(11):
            w_copy(h, index).wait_send()
        for index in (2, 3, 4, 5):
            d_copy(h, index).wait_send()


def shards(noise, keep):
    samples = noise[0, 0].T
    consts = tables()
    dma = pltpu.SemaphoreType.DMA
    result = pl.pallas_call(
        kernel,
        out_shape=jax.ShapeDtypeStruct((OUT, CH), F32),
        in_specs=[
            pl.BlockSpec(memory_space=pltpu.HBM)
            for i in range(2 + len(consts))
        ],
        out_specs=pl.BlockSpec(memory_space=pltpu.VMEM),
        scratch_shapes=[
            pltpu.VMEM(samples.shape, BF16),
            pltpu.VMEM((1, CH), jnp.int32),
            *[pltpu.VMEM(c.shape, BF16) for c in consts],
            dma((2 + len(consts),)),
            pltpu.VMEM((H, WIN, 2 * F, CP), BF16),
            pltpu.VMEM((WIN, 16, 128), BF16),
            pltpu.VMEM((128, CH), BF16),
            pltpu.VMEM((16, SLANES), BF16),
            pltpu.VMEM((WIN, 16, SLANES), BF16),
            pltpu.VMEM((2, WIN + 1, 16, F), BF16),
            pltpu.VMEM((2, WIN, 64, F), BF16),
            pltpu.VMEM((4, ROWS, WIN * 2 * F), BF16),
            pltpu.VMEM((4, 16, CH), F32),
            pltpu.VMEM((H, ROWS, CP), F32),
            pltpu.VMEM((H, 2, ROWS, CP), F32),
            pltpu.VMEM((H, 3, ROWS, CP), BF16),
            pltpu.VMEM((H, TOP, CP), BF16),
            pltpu.VMEM((H, ROWS - TOP, CP), BF16),
            pltpu.VMEM((H, ROWS, CP), BF16),
            pltpu.VMEM((H, ROWS, CP), BF16),
            dma((H, 11)),
            dma((H, 11)),
            dma((7,)),
            dma((7,)),
            dma((4,)),
            dma((WIN,)),
            dma((3,)),
            dma((2,)),
            dma((H, 6)),
            dma((H, 6)),
        ],
        compiler_params=pltpu.CompilerParams(
            collective_id=0, has_side_effects=True, vmem_limit_bytes=60 * 1024 * 1024
        ),
    )(samples, keep[0], *[jnp.asarray(c) for c in consts])
    return result[: GROUP * LAGS].reshape(LAGS, GROUP, CH).transpose(1, 0, 2)


def solution(mesh):
    in_specs = (P("day", "col", "row", None), P("day", "col", "row"))
    out_specs = P(("col", "day"), None, "row")
    return jax.shard_map(shards, mesh=mesh, in_specs=in_specs, out_specs=out_specs, check_vma=False)
```

```python
import functools
import math

import jax
import jax.numpy as jnp
import ml_dtypes
import numpy as np
from jax import lax
from jax.experimental import pallas as pl
from jax.experimental.pallas import tpu as pltpu
from jax.sharding import PartitionSpec as P

MESH = pl.DeviceIdType.MESH
BF16 = jnp.bfloat16
F32 = jnp.float32

F = 256
LOW = 60
HALF = 64
MAXLAG = 25
LAGS = 2 * MAXLAG + 1
TLEN = 1500
CH = 256
WIN = 8
GROUP = 4
HALFRANK = 16
RANK = 2 * HALFRANK
ROWS = GROUP * RANK
TOP = ROWS // 2
OUT = 208
SLANES = F + 128
H = 1
CP = CH // H
PARTS = 2
DP = CH // PARTS


def tables():
    k = np.arange(F)
    t = np.arange(TLEN)
    angle = 2.0 * np.pi / TLEN * ((LOW + k)[:, None] * t[None, :] % TLEN)
    twiddle = np.concatenate([np.cos(angle), -np.sin(angle)], axis=0).astype(np.float32)
    high = twiddle.astype(ml_dtypes.bfloat16)
    rest = (twiddle - high.astype(np.float32)).astype(ml_dtypes.bfloat16)
    band = (np.abs(k[:, None] - k[None, :]) <= HALF).astype(ml_dtypes.bfloat16)
    lag = np.arange(LAGS) - MAXLAG
    lag_angle = 2.0 * np.pi / TLEN * ((LOW + k)[None, :] * lag[:, None] % TLEN)
    back, basis = [], []
    for part in (np.cos(lag_angle), -np.sin(lag_angle)):
        left, size, right = np.linalg.svd(part, full_matrices=False)
        left, size, right = left[:, :HALFRANK], size[:HALFRANK], right[:HALFRANK]
        back.append(left * size / 16.0)
        basis.append(right * 16.0)
    basis = np.repeat(np.concatenate(basis), GROUP, axis=0).astype(ml_dtypes.bfloat16)
    synth = np.zeros((OUT, ROWS), np.float32)
    synth[: GROUP * LAGS] = np.kron(np.concatenate(back, axis=1), np.eye(GROUP))
    synth_high = synth.astype(ml_dtypes.bfloat16)
    synth_rest = (synth - synth_high.astype(np.float32)).astype(ml_dtypes.bfloat16)
    synth = np.concatenate([synth_high, synth_high, synth_rest], axis=1)
    rep = np.zeros((64, 16), ml_dtypes.bfloat16)
    for g in range(2):
        for part in range(2):
            for i in range(16):
                rep[g * 32 + part * 16 + i, part * 8 + g * GROUP + i % GROUP] = 1
    pick = np.zeros((16, CH), ml_dtypes.bfloat16)
    for i in range(16):
        pick[i, (i % 8) * 32] = 1
    return (
        high,
        rest,
        band,
        basis,
        synth,
        rep,
        pick,
    )


def kernel(
    noise_hbm, keep_hbm, high_hbm, rest_hbm, band_hbm, basis_hbm, synth_hbm, rep_hbm, pick_hbm, out,
    noise, keep, high, rest, band, basis, synth, rep, pick, load,
    wall, kept, marks, sown, held, sfin, spread, tmat, inverse, own, near, part, fold_up, fold_down, got_up, got_down,
    w_send, w_recv, k_send, k_recv, s_send, s_recv, t_send, t_recv, d_send, d_recv,
):
    loads = [
        pltpu.make_async_copy(src, dst, load.at[i])
        for i, (src, dst) in enumerate(
            [
                (noise_hbm, noise),
                (keep_hbm, keep),
                (high_hbm, high),
                (rest_hbm, rest),
                (band_hbm, band),
                (pick_hbm, pick),
                (rep_hbm, rep),
                (basis_hbm, basis),
                (synth_hbm, synth),
            ]
        )
    ]
    for copy in loads:
        copy.start()

    row, col, day = lax.axis_index("row"), lax.axis_index("col"), lax.axis_index("day")
    z, x = row // 4, row % 4
    y, core = col // 2, col % 2
    side = x % 2
    holder = core == x // 2
    home = jnp.logical_and(holder, y == z)
    away = jnp.logical_not(home)

    def column(step, flip=0):
        return ((y + step) % 4) * 2 + (core + flip) % 2

    upper, lower, far, sibling = column(1), column(3), column(2), column(0, 1)

    def device(r=row, c=col, d=day):
        return (r, c, d)

    def remote(src, dst, send, recv, target):
        return pltpu.make_async_remote_copy(
            src_ref=src, dst_ref=dst, send_sem=send, recv_sem=recv,
            device_id=target, device_id_type=MESH,
        )

    barrier = pltpu.get_barrier_semaphore()

    def greet(target):
        pl.semaphore_signal(barrier, inc=1, device_id=target, device_id_type=MESH)

    for i in range(1, 8):
        greet(device(c=(col + i) % 8))
    for i in (1, 3):
        greet(device(d=(day + i) % 4))
    @pl.when(holder)
    def _():
        for i in range(8):
            if i:
                greet(device(r=4 * y + x, c=(col + i) % 8))
            else:

                @pl.when(away)
                def _():
                    greet(device(r=4 * y + x))

    for e in range(2):

        @pl.when(x != 2 * core + e)
        def _():
            greet(device(r=4 * z + 2 * core + e))

    for copy in loads[:3]:
        copy.wait()
    spectrum = jnp.dot(high[...], noise[...], preferred_element_type=F32)
    loads[3].wait()
    spectrum += jnp.dot(rest[...], noise[...], preferred_element_type=F32)
    loads[4].wait()
    keep_row = keep[...].astype(F32)
    bins = lax.broadcasted_iota(jnp.int32, (F, CP), 0)
    count = jnp.minimum(bins + HALF, F - 1) - jnp.maximum(bins - HALF, 0) + 1
    weight = 1.0 / count.astype(F32)

    def whiten(h):
        cut = slice(h * CP, (h + 1) * CP)
        real, imag = spectrum[:F, cut], spectrum[F:, cut]
        magnitude = jnp.sqrt(real * real + imag * imag)
        total = jnp.dot(band[...], magnitude.astype(BF16), preferred_element_type=F32)
        scale = keep_row[:, cut] / (total * weight + 1e-6)
        white = jnp.concatenate([real * scale, imag * scale], axis=0).astype(BF16)
        wall[h, col] = white
        return white

    white = [whiten(0)]
    def s_copy(k):
        target = device(r=((z + k) % 4) * 4 + x, c=row // 2)
        return remote(sown, held.at[col], s_send.at[k], s_recv.at[col], target)

    def s_each(method):
        for k in (1, 2, 3):
            getattr(s_copy(k), method)()

        @pl.when(away)
        def _():
            getattr(s_copy(0), method)()

    def t_copy(i):
        ref = sfin.at[side]
        target = device(r=z * 4 + (x + i) % 4)
        return remote(ref, ref, t_send.at[i - 1], t_recv.at[side], target)

    def s_forward():
        @pl.when(holder)
        def _():
            for w in range(WIN):

                @pl.when(jnp.logical_not(home & (col == w)))
                def _():
                    remote(
                        sown, held.at[w], s_send.at[0], s_recv.at[w], device(c=sibling)
                    ).wait_recv()

            lane = lax.broadcasted_iota(jnp.int32, (16, 128), 1)
            mark = jnp.zeros((16, 128), F32)
            for w in range(WIN):
                sfin[side, w] = held[w, :, 0:F]
                mark = jnp.where(lane == w, held[w, :, F:].astype(F32), mark)
            sfin[side, WIN] = jnp.concatenate([mark, mark], axis=1).astype(BF16)

    def s_spread(e):
        @pl.when(holder & (side == e))
        def _():
            for i in (2, 1, 3):
                t_copy(i).start()

    def s_arrival(e):
        @pl.when(jnp.logical_not(holder & (side == e)))
        def _():
            ref = sfin.at[e]
            remote(ref, ref, t_send.at[0], t_recv.at[e], device(c=sibling)).wait_recv()

    top, bottom = (0, F), (F, F)

    def block(h, w, rows):
        if rows is None:
            return wall.at[h, w]
        return wall.at[h, w, pl.ds(rows[0], rows[1]), :]

    routes = [
        (col, top, upper, lower),
        (col, bottom, lower, upper),
        (col, bottom, upper, lower),
        (col, top, lower, upper),
        (col, None, sibling, sibling),
        (lower, top, upper, far),
        (upper, bottom, lower, far),
        (lower, None, sibling, column(3, 1)),
        (upper, None, sibling, column(1, 1)),
        (far, top, sibling, column(2, 1)),
        (far, bottom, sibling, column(2, 1)),
    ]

    def w_copy(h, index):
        w, rows, target, _ = routes[index]
        ref = block(h, w, rows)
        return remote(ref, ref, w_send.at[h, index], w_recv.at[h, index], device(c=target))

    def w_arrival(h, *indices):
        for index in indices:
            _, rows, _, w = routes[index]
            ref = block(h, w, rows)
            remote(
                ref, ref, w_send.at[h, index], w_recv.at[h, index], device(c=sibling)
            ).wait_recv()

    def w_start(h, *indices):
        for index in indices:
            w_copy(h, index).start()

    def k_copy(i):
        ref = kept.at[col]
        return remote(ref, ref, k_send.at[i - 1], k_recv.at[i - 1], device(c=(col + i) % 8))

    def first_hop(h):
        w_start(h, 0, 1)

    def rest_hop(h):
        w_start(h, 2, 3, 4)

    def second_hop(h):
        w_arrival(h, 0)
        w_start(h, 5)
        w_arrival(h, 1)
        w_start(h, 6)

    def third_hop(h):
        w_arrival(h, 2)
        w_start(h, 7)
        w_arrival(h, 3)
        w_start(h, 8)

    def fourth_hop(h):
        w_arrival(h, 5)
        w_start(h, 9)
        w_arrival(h, 6)
        w_start(h, 10)

    def last_hop(h):
        w_arrival(h, 4, 7, 8, 9, 10)

    def spread_sources(e):
        def body(w, carry):
            rows = jnp.dot(rep[...], sfin[e, w], preferred_element_type=F32)
            spread[e, w] = rows.astype(BF16)
            return carry

        lax.fori_loop(0, WIN, body, 0, unroll=4)

    def count_pairs(e):
        rows = jnp.dot(rep[...], sfin[e, WIN, :, 0:128], preferred_element_type=F32)
        pairs = jnp.dot(rows.astype(BF16), marks[...], preferred_element_type=F32)
        for g in range(2):
            floor = jnp.maximum(pairs[32 * g : 32 * g + 16], 1.0)
            inverse[2 * e + g] = (1.0 / math.sqrt(F)) / floor

    def make(slot, d):
        e, g = d // 2, d % 2
        real_rows = pl.ds(pl.multiple_of(32 * g, 32), 16)
        imag_rows = pl.ds(pl.multiple_of(32 * g + 16, 16), 16)

        def body(w, carry):
            s_real = spread[e, w, real_rows, :]
            s_imag = spread[e, w, imag_rows, :]
            at = pl.multiple_of(w * 2 * F, 2 * F)
            for t in range(ROWS // 16):
                rows = slice(16 * t, 16 * t + 16)
                table = basis[rows, :]
                first, second = (s_real, s_imag) if 2 * t < ROWS // 16 else (-s_imag, s_real)
                tmat[slot, rows, pl.ds(at, F)] = first * table
                tmat[slot, rows, pl.ds(at + F, F)] = second * table
            return carry

        lax.fori_loop(0, WIN, body, 0)

    def partial(p, slot, d):
        cut = slice(p * DP, (p + 1) * DP)
        value = jnp.dot(
            tmat[slot], wall[0, :, :, cut].reshape(WIN * 2 * F, DP), preferred_element_type=F32
        )
        factor = inverse[d, :, cut]
        return (value.reshape(ROWS // 16, 16, DP) * factor[None]).reshape(ROWS, DP)

    up, down, away_day = (day + 1) % 4, (day + 3) % 4, (day + 2) % 4
    head, tail = pl.ds(0, TOP), pl.ds(TOP, ROWS - TOP)

    def d_copy(h, index):
        src, dst, target = [
            (part.at[h, 0, head, :], fold_up.at[h], up),
            (part.at[h, 0, tail, :], fold_down.at[h], down),
            (part.at[h, 1, tail, :], got_up.at[h, tail, :], up),
            (part.at[h, 2, head, :], got_down.at[h, head, :], down),
            (part.at[h, 1, head, :], got_up.at[h, head, :], up),
            (part.at[h, 2, tail, :], got_down.at[h, tail, :], down),
        ][index]
        return remote(src, dst, d_send.at[h, index], d_recv.at[h, index], device(d=target))

    def send_far(h):
        part[h, 0] = partial(h, 0, away_day).astype(BF16)
        d_copy(h, 0).start()
        d_copy(h, 1).start()

    def compute_near(h):
        plus = partial(h, 1, up)
        near[h, 0] = plus
        part[h, 1, TOP:, :] = plus[TOP:].astype(BF16)
        minus = partial(h, 2, down)
        near[h, 1] = minus
        part[h, 2, 0:TOP, :] = minus[:TOP].astype(BF16)

    def send_near(h):
        d_copy(h, 2).start()
        d_copy(h, 3).start()

    def send_folded(h):
        d_copy(h, 0).wait_recv()
        part[h, 1, 0:TOP, :] = (near[h, 0, 0:TOP, :] + fold_up[h].astype(F32)).astype(BF16)
        d_copy(h, 4).start()
        d_copy(h, 1).wait_recv()
        part[h, 2, TOP:, :] = (near[h, 1, TOP:, :] + fold_down[h].astype(F32)).astype(BF16)
        d_copy(h, 5).start()

    def finish(h):
        for index in (2, 3, 4, 5):
            d_copy(h, index).wait_recv()
        result = own[h] + got_up[h].astype(F32) + got_down[h].astype(F32)
        high_part = result.astype(BF16)
        rest_part = (result - high_part.astype(F32)).astype(BF16)
        out[:, h * DP : (h + 1) * DP] = jnp.dot(
            synth[...],
            jnp.concatenate([high_part, rest_part, high_part]),
            preferred_element_type=F32,
        )

    def k_arrival():
        for i in range(1, 8):
            ref = kept.at[(col + 8 - i) % 8]
            remote(ref, ref, k_send.at[i - 1], k_recv.at[i - 1], device(c=sibling)).wait_recv()
        rows = [
            jnp.concatenate([kept[w, 0:1, :], kept[w, 8:9, :]], axis=1).astype(F32)
            for w in range(WIN)
        ]
        marks[0:16, :] = jnp.concatenate(rows + [jnp.zeros((8, CH), F32)]).astype(BF16)

    first_side = away_day // 2
    pl.semaphore_wait(barrier, 7 + 2 + 3 + away.astype(jnp.int32) + 3 * holder.astype(jnp.int32))
    first_hop(0)
    kept[col] = jnp.concatenate(
        [jnp.broadcast_to(keep_row[:, :128], (8, 128)), jnp.broadcast_to(keep_row[:, 128:], (8, 128))]
    ).astype(BF16)
    marks[...] = jnp.zeros_like(marks)

    loads[5].wait()
    picked = jnp.zeros((16, 2 * F), F32)
    for h in range(H):
        picked += lax.dot_general(
            pick[:, h * CP : (h + 1) * CP],
            white[h],
            (((1,), (1,)), ((), ())),
            preferred_element_type=F32,
        )
    lower_half = lax.broadcasted_iota(jnp.int32, (16, F), 0) < 8
    mixed = jnp.where(lower_half, picked[:, :F], picked[:, F:])
    flag = jnp.sum(pick[...].astype(F32) * keep_row, axis=1, keepdims=True)
    message = jnp.concatenate([mixed, jnp.broadcast_to(flag, (16, 128))], axis=1).astype(BF16)
    sown[...] = message

    @pl.when(home)
    def _():
        held[col] = message
    s_each("start")
    for i in range(1, 8):
        k_copy(i).start()
    rest_hop(0)
    second_hop(0)
    s_forward()
    s_spread(first_side)
    s_spread(1 - first_side)
    third_hop(0)
    for copy in loads[6:]:
        copy.wait()
    k_arrival()
    s_arrival(first_side)
    spread_sources(first_side)
    make(0, away_day)
    fourth_hop(0)
    s_arrival(1 - first_side)
    spread_sources(1 - first_side)
    count_pairs(first_side)
    count_pairs(1 - first_side)
    make(1, up)
    make(2, down)
    last_hop(0)
    send_far(0)
    send_far(1)
    compute_near(0)
    send_near(0)
    compute_near(1)
    send_near(1)
    make(3, day)
    own[0] = partial(0, 3, day)
    own[1] = partial(1, 3, day)
    send_folded(0)
    send_folded(1)
    finish(0)
    finish(1)

    s_each("wait_send")

    @pl.when(holder)
    def _():
        for i in (1, 2, 3):
            t_copy(i).wait_send()

    for i in range(1, 8):
        k_copy(i).wait_send()
    for h in range(H):
        for index in range(11):
            w_copy(h, index).wait_send()
    for p in range(PARTS):
        for index in range(6):
            d_copy(p, index).wait_send()


def shards(noise, keep):
    samples = noise[0, 0].T
    consts = tables()
    dma = pltpu.SemaphoreType.DMA
    result = pl.pallas_call(
        kernel,
        out_shape=jax.ShapeDtypeStruct((OUT, CH), F32),
        in_specs=[
            pl.BlockSpec(memory_space=pltpu.HBM)
            for i in range(2 + len(consts))
        ],
        out_specs=pl.BlockSpec(memory_space=pltpu.VMEM),
        scratch_shapes=[
            pltpu.VMEM(samples.shape, BF16),
            pltpu.VMEM((1, CH), jnp.int32),
            *[pltpu.VMEM(c.shape, BF16) for c in consts],
            dma((2 + len(consts),)),
            pltpu.VMEM((H, WIN, 2 * F, CP), BF16),
            pltpu.VMEM((WIN, 16, 128), BF16),
            pltpu.VMEM((128, CH), BF16),
            pltpu.VMEM((16, SLANES), BF16),
            pltpu.VMEM((WIN, 16, SLANES), BF16),
            pltpu.VMEM((2, WIN + 1, 16, F), BF16),
            pltpu.VMEM((2, WIN, 64, F), BF16),
            pltpu.VMEM((4, ROWS, WIN * 2 * F), BF16),
            pltpu.VMEM((4, 16, CH), F32),
            pltpu.VMEM((PARTS, ROWS, DP), F32),
            pltpu.VMEM((PARTS, 2, ROWS, DP), F32),
            pltpu.VMEM((PARTS, 3, ROWS, DP), BF16),
            pltpu.VMEM((PARTS, TOP, DP), BF16),
            pltpu.VMEM((PARTS, ROWS - TOP, DP), BF16),
            pltpu.VMEM((PARTS, ROWS, DP), BF16),
            pltpu.VMEM((PARTS, ROWS, DP), BF16),
            dma((H, 11)),
            dma((H, 11)),
            dma((7,)),
            dma((7,)),
            dma((4,)),
            dma((WIN,)),
            dma((3,)),
            dma((2,)),
            dma((PARTS, 6)),
            dma((PARTS, 6)),
        ],
        compiler_params=pltpu.CompilerParams(
            collective_id=0, has_side_effects=True, vmem_limit_bytes=60 * 1024 * 1024
        ),
    )(samples, keep[0], *[jnp.asarray(c) for c in consts])
    return result[: GROUP * LAGS].reshape(LAGS, GROUP, CH).transpose(1, 0, 2)


def solution(mesh):
    in_specs = (P("day", "col", "row", None), P("day", "col", "row"))
    out_specs = P(("col", "day"), None, "row")
    return jax.shard_map(shards, mesh=mesh, in_specs=in_specs, out_specs=out_specs, check_vma=False)
```

```python
import functools
import math

import jax
import jax.numpy as jnp
import ml_dtypes
import numpy as np
from jax import lax
from jax.experimental import pallas as pl
from jax.experimental.pallas import tpu as pltpu
from jax.sharding import PartitionSpec as P

MESH = pl.DeviceIdType.MESH
BF16 = jnp.bfloat16
F32 = jnp.float32

F = 256
LOW = 60
HALF = 64
MAXLAG = 25
LAGS = 2 * MAXLAG + 1
TLEN = 1500
CH = 256
WIN = 8
GROUP = 4
HALFRANK = 16
RANK = 2 * HALFRANK
ROWS = GROUP * RANK
TOP = ROWS // 2
OUT = 208
SLANES = F + 128
H = 1
CP = CH // H
PARTS = 2
DP = CH // PARTS


def tables():
    k = np.arange(F)
    t = np.arange(TLEN)
    angle = 2.0 * np.pi / TLEN * ((LOW + k)[:, None] * t[None, :] % TLEN)
    twiddle = np.concatenate([np.cos(angle), -np.sin(angle)], axis=0).astype(np.float32)
    high = twiddle.astype(ml_dtypes.bfloat16)
    rest = (twiddle - high.astype(np.float32)).astype(ml_dtypes.bfloat16)
    band = (np.abs(k[:, None] - k[None, :]) <= HALF).astype(ml_dtypes.bfloat16)
    lag = np.arange(LAGS) - MAXLAG
    lag_angle = 2.0 * np.pi / TLEN * ((LOW + k)[None, :] * lag[:, None] % TLEN)
    back, basis = [], []
    for part in (np.cos(lag_angle), -np.sin(lag_angle)):
        left, size, right = np.linalg.svd(part, full_matrices=False)
        left, size, right = left[:, :HALFRANK], size[:HALFRANK], right[:HALFRANK]
        back.append(left * size / 16.0)
        basis.append(right * 16.0)
    basis = np.repeat(np.concatenate(basis), GROUP, axis=0).astype(ml_dtypes.bfloat16)
    synth = np.zeros((OUT, ROWS), np.float32)
    synth[: GROUP * LAGS] = np.kron(np.concatenate(back, axis=1), np.eye(GROUP))
    synth_high = synth.astype(ml_dtypes.bfloat16)
    synth_rest = (synth - synth_high.astype(np.float32)).astype(ml_dtypes.bfloat16)
    terms = np.concatenate([synth_high, synth_high, synth_rest], axis=1)
    synth = np.zeros((LAGS, PARTS, GROUP, PARTS, terms.shape[1]), terms.dtype)
    for p in range(PARTS):
        synth[:, p, :, p] = terms[: GROUP * LAGS].reshape(LAGS, GROUP, -1)
    synth = synth.reshape(LAGS * PARTS * GROUP, -1)
    rep = np.zeros((64, 16), ml_dtypes.bfloat16)
    for g in range(2):
        for part in range(2):
            for i in range(16):
                rep[g * 32 + part * 16 + i, part * 8 + g * GROUP + i % GROUP] = 1
    pick = np.zeros((16, CH), ml_dtypes.bfloat16)
    for i in range(16):
        pick[i, (i % 8) * 32] = 1
    return (
        high,
        rest,
        band,
        basis,
        synth,
        rep,
        pick,
    )


def kernel(
    noise_hbm, keep_hbm, high_hbm, rest_hbm, band_hbm, basis_hbm, synth_hbm, rep_hbm, pick_hbm, out,
    noise, keep, high, rest, band, basis, synth, rep, pick, load,
    wall, kept, marks, sown, held, sfin, spread, tmat, inverse, own, near, part, fold_up, fold_down, got_up, got_down,
    w_send, w_recv, k_send, k_recv, s_send, s_recv, t_send, t_recv, d_send, d_recv,
):
    loads = [
        pltpu.make_async_copy(src, dst, load.at[i])
        for i, (src, dst) in enumerate(
            [
                (noise_hbm, noise),
                (keep_hbm, keep),
                (high_hbm, high),
                (rest_hbm, rest),
                (band_hbm, band),
                (pick_hbm, pick),
                (rep_hbm, rep),
                (basis_hbm, basis),
                (synth_hbm, synth),
            ]
        )
    ]
    for copy in loads:
        copy.start()

    row, col, day = lax.axis_index("row"), lax.axis_index("col"), lax.axis_index("day")
    z, x = row // 4, row % 4
    y, core = col // 2, col % 2
    side = x % 2
    holder = core == x // 2
    home = jnp.logical_and(holder, y == z)
    away = jnp.logical_not(home)

    def column(step, flip=0):
        return ((y + step) % 4) * 2 + (core + flip) % 2

    upper, lower, far, sibling = column(1), column(3), column(2), column(0, 1)

    def device(r=row, c=col, d=day):
        return (r, c, d)

    def remote(src, dst, send, recv, target):
        return pltpu.make_async_remote_copy(
            src_ref=src, dst_ref=dst, send_sem=send, recv_sem=recv,
            device_id=target, device_id_type=MESH,
        )

    barrier = pltpu.get_barrier_semaphore()

    def greet(target):
        pl.semaphore_signal(barrier, inc=1, device_id=target, device_id_type=MESH)

    for i in range(1, 8):
        greet(device(c=(col + i) % 8))
    for i in (1, 3):
        greet(device(d=(day + i) % 4))
    @pl.when(holder)
    def _():
        for i in range(8):
            if i:
                greet(device(r=4 * y + x, c=(col + i) % 8))
            else:

                @pl.when(away)
                def _():
                    greet(device(r=4 * y + x))

    for e in range(2):

        @pl.when(x != 2 * core + e)
        def _():
            greet(device(r=4 * z + 2 * core + e))

    for copy in loads[:3]:
        copy.wait()
    spectrum = jnp.dot(high[...], noise[...], preferred_element_type=F32)
    loads[3].wait()
    spectrum += jnp.dot(rest[...], noise[...], preferred_element_type=F32)
    loads[4].wait()
    keep_row = keep[...].astype(F32)
    bins = lax.broadcasted_iota(jnp.int32, (F, CP), 0)
    count = jnp.minimum(bins + HALF, F - 1) - jnp.maximum(bins - HALF, 0) + 1
    weight = 1.0 / count.astype(F32)

    def whiten(h):
        cut = slice(h * CP, (h + 1) * CP)
        real, imag = spectrum[:F, cut], spectrum[F:, cut]
        magnitude = jnp.sqrt(real * real + imag * imag)
        total = jnp.dot(band[...], magnitude.astype(BF16), preferred_element_type=F32)
        scale = keep_row[:, cut] / (total * weight + 1e-6)
        white = jnp.concatenate([real * scale, imag * scale], axis=0).astype(BF16)
        wall[h, col] = white
        return white

    white = [whiten(0)]
    def s_copy(k):
        target = device(r=((z + k) % 4) * 4 + x, c=row // 2)
        return remote(sown, held.at[col], s_send.at[k], s_recv.at[col], target)

    def s_each(method):
        for k in (1, 2, 3):
            getattr(s_copy(k), method)()

        @pl.when(away)
        def _():
            getattr(s_copy(0), method)()

    def t_copy(i):
        ref = sfin.at[side]
        target = device(r=z * 4 + (x + i) % 4)
        return remote(ref, ref, t_send.at[i - 1], t_recv.at[side], target)

    def s_forward():
        @pl.when(holder)
        def _():
            for w in range(WIN):

                @pl.when(jnp.logical_not(home & (col == w)))
                def _():
                    remote(
                        sown, held.at[w], s_send.at[0], s_recv.at[w], device(c=sibling)
                    ).wait_recv()

            lane = lax.broadcasted_iota(jnp.int32, (16, 128), 1)
            mark = jnp.zeros((16, 128), F32)
            for w in range(WIN):
                sfin[side, w] = held[w, :, 0:F]
                mark = jnp.where(lane == w, held[w, :, F:].astype(F32), mark)
            sfin[side, WIN] = jnp.concatenate([mark, mark], axis=1).astype(BF16)

    def s_spread(e):
        @pl.when(holder & (side == e))
        def _():
            for i in (2, 1, 3):
                t_copy(i).start()

    def s_arrival(e):
        @pl.when(jnp.logical_not(holder & (side == e)))
        def _():
            ref = sfin.at[e]
            remote(ref, ref, t_send.at[0], t_recv.at[e], device(c=sibling)).wait_recv()

    top, bottom = (0, F), (F, F)

    def block(h, w, rows):
        if rows is None:
            return wall.at[h, w]
        return wall.at[h, w, pl.ds(rows[0], rows[1]), :]

    routes = [
        (col, top, upper, lower),
        (col, bottom, lower, upper),
        (col, bottom, upper, lower),
        (col, top, lower, upper),
        (col, None, sibling, sibling),
        (lower, top, upper, far),
        (upper, bottom, lower, far),
        (lower, None, sibling, column(3, 1)),
        (upper, None, sibling, column(1, 1)),
        (far, top, sibling, column(2, 1)),
        (far, bottom, sibling, column(2, 1)),
    ]

    def w_copy(h, index):
        w, rows, target, _ = routes[index]
        ref = block(h, w, rows)
        return remote(ref, ref, w_send.at[h, index], w_recv.at[h, index], device(c=target))

    def w_arrival(h, *indices):
        for index in indices:
            _, rows, _, w = routes[index]
            ref = block(h, w, rows)
            remote(
                ref, ref, w_send.at[h, index], w_recv.at[h, index], device(c=sibling)
            ).wait_recv()

    def w_start(h, *indices):
        for index in indices:
            w_copy(h, index).start()

    def k_copy(i):
        ref = kept.at[col]
        return remote(ref, ref, k_send.at[i - 1], k_recv.at[i - 1], device(c=(col + i) % 8))

    def first_hop(h):
        w_start(h, 0, 1)

    def rest_hop(h):
        w_start(h, 2, 3, 4)

    def second_hop(h):
        w_arrival(h, 0)
        w_start(h, 5)
        w_arrival(h, 1)
        w_start(h, 6)

    def third_hop(h):
        w_arrival(h, 2)
        w_start(h, 7)
        w_arrival(h, 3)
        w_start(h, 8)

    def fourth_hop(h):
        w_arrival(h, 5)
        w_start(h, 9)
        w_arrival(h, 6)
        w_start(h, 10)

    def last_hop(h):
        w_arrival(h, 4, 7, 8, 9, 10)

    def spread_sources(e):
        def body(w, carry):
            rows = jnp.dot(rep[...], sfin[e, w], preferred_element_type=F32)
            spread[e, w] = rows.astype(BF16)
            return carry

        lax.fori_loop(0, WIN, body, 0, unroll=4)

    def count_pairs(e):
        rows = jnp.dot(rep[...], sfin[e, WIN, :, 0:128], preferred_element_type=F32)
        pairs = jnp.dot(rows.astype(BF16), marks[...], preferred_element_type=F32)
        for g in range(2):
            floor = jnp.maximum(pairs[32 * g : 32 * g + 16], 1.0)
            inverse[2 * e + g] = (1.0 / math.sqrt(F)) / floor

    def make(slot, d):
        e, g = d // 2, d % 2
        real_rows = pl.ds(pl.multiple_of(32 * g, 32), 16)
        imag_rows = pl.ds(pl.multiple_of(32 * g + 16, 16), 16)

        def body(w, carry):
            s_real = spread[e, w, real_rows, :]
            s_imag = spread[e, w, imag_rows, :]
            at = pl.multiple_of(w * 2 * F, 2 * F)
            for t in range(ROWS // 16):
                rows = slice(16 * t, 16 * t + 16)
                table = basis[rows, :]
                first, second = (s_real, s_imag) if 2 * t < ROWS // 16 else (-s_imag, s_real)
                tmat[slot, rows, pl.ds(at, F)] = first * table
                tmat[slot, rows, pl.ds(at + F, F)] = second * table
            return carry

        lax.fori_loop(0, WIN, body, 0)

    def partial(p, slot, d):
        cut = slice(p * DP, (p + 1) * DP)
        value = jnp.dot(
            tmat[slot], wall[0, :, :, cut].reshape(WIN * 2 * F, DP), preferred_element_type=F32
        )
        factor = inverse[d, :, cut]
        return (value.reshape(ROWS // 16, 16, DP) * factor[None]).reshape(ROWS, DP)

    up, down, away_day = (day + 1) % 4, (day + 3) % 4, (day + 2) % 4
    head, tail = pl.ds(0, TOP), pl.ds(TOP, ROWS - TOP)

    def d_copy(h, index):
        src, dst, target = [
            (part.at[h, 0, head, :], fold_up.at[h], up),
            (part.at[h, 0, tail, :], fold_down.at[h], down),
            (part.at[h, 1, tail, :], got_up.at[h, tail, :], up),
            (part.at[h, 2, head, :], got_down.at[h, head, :], down),
            (part.at[h, 1, head, :], got_up.at[h, head, :], up),
            (part.at[h, 2, tail, :], got_down.at[h, tail, :], down),
        ][index]
        return remote(src, dst, d_send.at[h, index], d_recv.at[h, index], device(d=target))

    def send_far(h):
        part[h, 0] = partial(h, 0, away_day).astype(BF16)
        d_copy(h, 0).start()
        d_copy(h, 1).start()

    def compute_near(h):
        plus = partial(h, 1, up)
        near[h, 0] = plus
        part[h, 1, TOP:, :] = plus[TOP:].astype(BF16)
        minus = partial(h, 2, down)
        near[h, 1] = minus
        part[h, 2, 0:TOP, :] = minus[:TOP].astype(BF16)

    def send_near(h):
        d_copy(h, 2).start()
        d_copy(h, 3).start()

    def send_folded(h):
        d_copy(h, 0).wait_recv()
        part[h, 1, 0:TOP, :] = (near[h, 0, 0:TOP, :] + fold_up[h].astype(F32)).astype(BF16)
        d_copy(h, 4).start()
        d_copy(h, 1).wait_recv()
        part[h, 2, TOP:, :] = (near[h, 1, TOP:, :] + fold_down[h].astype(F32)).astype(BF16)
        d_copy(h, 5).start()

    def finish(h):
        for index in (2, 3, 4, 5):
            d_copy(h, index).wait_recv()
        result = own[h] + got_up[h].astype(F32) + got_down[h].astype(F32)
        high_part = result.astype(BF16)
        rest_part = (result - high_part.astype(F32)).astype(BF16)
        return [high_part, rest_part, high_part]

    def k_arrival():
        for i in range(1, 8):
            ref = kept.at[(col + 8 - i) % 8]
            remote(ref, ref, k_send.at[i - 1], k_recv.at[i - 1], device(c=sibling)).wait_recv()
        rows = [
            jnp.concatenate([kept[w, 0:1, :], kept[w, 8:9, :]], axis=1).astype(F32)
            for w in range(WIN)
        ]
        marks[0:16, :] = jnp.concatenate(rows + [jnp.zeros((8, CH), F32)]).astype(BF16)

    first_side = away_day // 2
    pl.semaphore_wait(barrier, 7 + 2 + 3 + away.astype(jnp.int32) + 3 * holder.astype(jnp.int32))
    first_hop(0)
    kept[col] = jnp.concatenate(
        [jnp.broadcast_to(keep_row[:, :128], (8, 128)), jnp.broadcast_to(keep_row[:, 128:], (8, 128))]
    ).astype(BF16)
    marks[...] = jnp.zeros_like(marks)

    loads[5].wait()
    picked = jnp.zeros((16, 2 * F), F32)
    for h in range(H):
        picked += lax.dot_general(
            pick[:, h * CP : (h + 1) * CP],
            white[h],
            (((1,), (1,)), ((), ())),
            preferred_element_type=F32,
        )
    lower_half = lax.broadcasted_iota(jnp.int32, (16, F), 0) < 8
    mixed = jnp.where(lower_half, picked[:, :F], picked[:, F:])
    flag = jnp.sum(pick[...].astype(F32) * keep_row, axis=1, keepdims=True)
    message = jnp.concatenate([mixed, jnp.broadcast_to(flag, (16, 128))], axis=1).astype(BF16)
    sown[...] = message

    @pl.when(home)
    def _():
        held[col] = message
    s_each("start")
    for i in range(1, 8):
        k_copy(i).start()
    rest_hop(0)
    second_hop(0)
    s_forward()
    s_spread(first_side)
    third_hop(0)
    s_spread(1 - first_side)
    for copy in loads[6:]:
        copy.wait()
    fourth_hop(0)
    k_arrival()
    s_arrival(first_side)
    spread_sources(first_side)
    make(0, away_day)
    count_pairs(first_side)
    last_hop(0)
    send_far(0)
    send_far(1)
    s_arrival(1 - first_side)
    spread_sources(1 - first_side)
    count_pairs(1 - first_side)
    make(1, up)
    make(2, down)
    compute_near(0)
    send_near(0)
    compute_near(1)
    send_near(1)
    make(3, day)
    own[0] = partial(0, 3, day)
    own[1] = partial(1, 3, day)
    send_folded(0)
    send_folded(1)
    terms = finish(0) + finish(1)
    out[...] = jnp.dot(synth[...], jnp.concatenate(terms), preferred_element_type=F32)

    s_each("wait_send")

    @pl.when(holder)
    def _():
        for i in (1, 2, 3):
            t_copy(i).wait_send()

    for i in range(1, 8):
        k_copy(i).wait_send()
    for h in range(H):
        for index in range(11):
            w_copy(h, index).wait_send()
    for p in range(PARTS):
        for index in range(6):
            d_copy(p, index).wait_send()


def shards(noise, keep):
    samples = noise[0, 0].T
    consts = tables()
    dma = pltpu.SemaphoreType.DMA
    result = pl.pallas_call(
        kernel,
        out_shape=jax.ShapeDtypeStruct((LAGS * PARTS * GROUP, DP), F32),
        in_specs=[
            pl.BlockSpec(memory_space=pltpu.HBM)
            for i in range(2 + len(consts))
        ],
        out_specs=pl.BlockSpec(memory_space=pltpu.VMEM),
        scratch_shapes=[
            pltpu.VMEM(samples.shape, BF16),
            pltpu.VMEM((1, CH), jnp.int32),
            *[pltpu.VMEM(c.shape, BF16) for c in consts],
            dma((2 + len(consts),)),
            pltpu.VMEM((H, WIN, 2 * F, CP), BF16),
            pltpu.VMEM((WIN, 16, 128), BF16),
            pltpu.VMEM((128, CH), BF16),
            pltpu.VMEM((16, SLANES), BF16),
            pltpu.VMEM((WIN, 16, SLANES), BF16),
            pltpu.VMEM((2, WIN + 1, 16, F), BF16),
            pltpu.VMEM((2, WIN, 64, F), BF16),
            pltpu.VMEM((4, ROWS, WIN * 2 * F), BF16),
            pltpu.VMEM((4, 16, CH), F32),
            pltpu.VMEM((PARTS, ROWS, DP), F32),
            pltpu.VMEM((PARTS, 2, ROWS, DP), F32),
            pltpu.VMEM((PARTS, 3, ROWS, DP), BF16),
            pltpu.VMEM((PARTS, TOP, DP), BF16),
            pltpu.VMEM((PARTS, ROWS - TOP, DP), BF16),
            pltpu.VMEM((PARTS, ROWS, DP), BF16),
            pltpu.VMEM((PARTS, ROWS, DP), BF16),
            dma((H, 11)),
            dma((H, 11)),
            dma((7,)),
            dma((7,)),
            dma((4,)),
            dma((WIN,)),
            dma((3,)),
            dma((2,)),
            dma((PARTS, 6)),
            dma((PARTS, 6)),
        ],
        compiler_params=pltpu.CompilerParams(
            collective_id=0, has_side_effects=True, vmem_limit_bytes=60 * 1024 * 1024
        ),
    )(samples, keep[0], *[jnp.asarray(c) for c in consts])
    return result.reshape(LAGS, PARTS, GROUP, DP).transpose(2, 0, 1, 3).reshape(GROUP, LAGS, CH)


def solution(mesh):
    in_specs = (P("day", "col", "row", None), P("day", "col", "row"))
    out_specs = P(("col", "day"), None, "row")
    return jax.shard_map(shards, mesh=mesh, in_specs=in_specs, out_specs=out_specs, check_vma=False)
```

```python
import functools
import math

import jax
import jax.numpy as jnp
import ml_dtypes
import numpy as np
from jax import lax
from jax.experimental import pallas as pl
from jax.experimental.pallas import tpu as pltpu
from jax.sharding import PartitionSpec as P

MESH = pl.DeviceIdType.MESH
BF16 = jnp.bfloat16
F32 = jnp.float32

F = 256
LOW = 60
HALF = 64
MAXLAG = 25
LAGS = 2 * MAXLAG + 1
TLEN = 1500
CH = 256
WIN = 8
GROUP = 4
HALFRANK = 16
RANK = 2 * HALFRANK
ROWS = GROUP * RANK
TOP = ROWS // 2
OUT = 208
SLANES = F + 128
H = 1
CP = CH // H
PARTS = 2
DP = CH // PARTS


def tables():
    k = np.arange(F)
    t = np.arange(TLEN)
    angle = 2.0 * np.pi / TLEN * ((LOW + k)[:, None] * t[None, :] % TLEN)
    twiddle = np.concatenate([np.cos(angle), -np.sin(angle)], axis=0).astype(np.float32)
    high = twiddle.astype(ml_dtypes.bfloat16)
    rest = (twiddle - high.astype(np.float32)).astype(ml_dtypes.bfloat16)
    band = (np.abs(k[:, None] - k[None, :]) <= HALF).astype(ml_dtypes.bfloat16)
    lag = np.arange(LAGS) - MAXLAG
    lag_angle = 2.0 * np.pi / TLEN * ((LOW + k)[None, :] * lag[:, None] % TLEN)
    back, basis = [], []
    for part in (np.cos(lag_angle), -np.sin(lag_angle)):
        left, size, right = np.linalg.svd(part, full_matrices=False)
        left, size, right = left[:, :HALFRANK], size[:HALFRANK], right[:HALFRANK]
        back.append(left * size / 16.0)
        basis.append(right * 16.0)
    basis = np.repeat(np.concatenate(basis), GROUP, axis=0).astype(ml_dtypes.bfloat16)
    synth = np.zeros((OUT, ROWS), np.float32)
    synth[: GROUP * LAGS] = np.kron(np.concatenate(back, axis=1), np.eye(GROUP))
    synth_high = synth.astype(ml_dtypes.bfloat16)
    synth_rest = (synth - synth_high.astype(np.float32)).astype(ml_dtypes.bfloat16)
    terms = np.concatenate([synth_high, synth_high, synth_rest], axis=1)
    synth = np.zeros((LAGS, PARTS, GROUP, PARTS, terms.shape[1]), terms.dtype)
    for p in range(PARTS):
        synth[:, p, :, p] = terms[: GROUP * LAGS].reshape(LAGS, GROUP, -1)
    synth = synth.reshape(LAGS * PARTS * GROUP, -1)
    rep = np.zeros((64, 16), ml_dtypes.bfloat16)
    for g in range(2):
        for part in range(2):
            for i in range(16):
                rep[g * 32 + part * 16 + i, part * 8 + g * GROUP + i % GROUP] = 1
    pick = np.zeros((16, CH), ml_dtypes.bfloat16)
    for i in range(16):
        pick[i, (i % 8) * 32] = 1
    return (
        high,
        rest,
        band,
        basis,
        synth,
        rep,
        pick,
    )


def kernel(
    noise_hbm, keep_hbm, high_hbm, rest_hbm, band_hbm, basis_hbm, synth_hbm, rep_hbm, pick_hbm, out,
    noise, keep, high, rest, band, basis, synth, rep, pick, load,
    wall, kept, marks, sown, held, sfin, spread, tmat, inverse, own, near, part, fold_up, fold_down, got_up, got_down,
    w_send, w_recv, k_send, k_recv, s_send, s_recv, t_send, t_recv, d_send, d_recv,
):
    loads = [
        pltpu.make_async_copy(src, dst, load.at[i])
        for i, (src, dst) in enumerate(
            [
                (noise_hbm, noise),
                (keep_hbm, keep),
                (high_hbm, high),
                (rest_hbm, rest),
                (band_hbm, band),
                (pick_hbm, pick),
                (rep_hbm, rep),
                (basis_hbm, basis),
                (synth_hbm, synth),
            ]
        )
    ]
    for copy in loads[:3]:
        copy.start()

    row, col, day = lax.axis_index("row"), lax.axis_index("col"), lax.axis_index("day")
    z, x = row // 4, row % 4
    y, core = col // 2, col % 2
    side = x % 2
    holder = core == x // 2
    home = jnp.logical_and(holder, y == z)
    away = jnp.logical_not(home)

    def column(step, flip=0):
        return ((y + step) % 4) * 2 + (core + flip) % 2

    upper, lower, far, sibling = column(1), column(3), column(2), column(0, 1)

    def device(r=row, c=col, d=day):
        return (r, c, d)

    def remote(src, dst, send, recv, target):
        return pltpu.make_async_remote_copy(
            src_ref=src, dst_ref=dst, send_sem=send, recv_sem=recv,
            device_id=target, device_id_type=MESH,
        )

    barrier = pltpu.get_barrier_semaphore()

    def greet(target):
        pl.semaphore_signal(barrier, inc=1, device_id=target, device_id_type=MESH)

    for i in range(1, 8):
        greet(device(c=(col + i) % 8))
    for i in (1, 3):
        greet(device(d=(day + i) % 4))
    @pl.when(holder)
    def _():
        for i in range(8):
            if i:
                greet(device(r=4 * y + x, c=(col + i) % 8))
            else:

                @pl.when(away)
                def _():
                    greet(device(r=4 * y + x))

    for e in range(2):

        @pl.when(x != 2 * core + e)
        def _():
            greet(device(r=4 * z + 2 * core + e))

    for copy in loads[3:]:
        copy.start()
    for copy in loads[:3]:
        copy.wait()
    spectrum = jnp.dot(high[...], noise[...], preferred_element_type=F32)
    loads[3].wait()
    spectrum += jnp.dot(rest[...], noise[...], preferred_element_type=F32)
    loads[4].wait()
    keep_row = keep[...].astype(F32)
    bins = lax.broadcasted_iota(jnp.int32, (F, CP), 0)
    count = jnp.minimum(bins + HALF, F - 1) - jnp.maximum(bins - HALF, 0) + 1
    weight = 1.0 / count.astype(F32)

    def whiten(h):
        cut = slice(h * CP, (h + 1) * CP)
        real, imag = spectrum[:F, cut], spectrum[F:, cut]
        magnitude = jnp.sqrt(real * real + imag * imag)
        total = jnp.dot(band[...], magnitude.astype(BF16), preferred_element_type=F32)
        scale = keep_row[:, cut] / (total * weight + 1e-6)
        white = jnp.concatenate([real * scale, imag * scale], axis=0).astype(BF16)
        wall[h, col] = white
        return white

    white = [whiten(0)]
    def s_copy(k):
        target = device(r=((z + k) % 4) * 4 + x, c=row // 2)
        return remote(sown, held.at[col], s_send.at[k], s_recv.at[col], target)

    def s_each(method):
        for k in (1, 2, 3):
            getattr(s_copy(k), method)()

        @pl.when(away)
        def _():
            getattr(s_copy(0), method)()

    def t_copy(i):
        ref = sfin.at[side]
        target = device(r=z * 4 + (x + i) % 4)
        return remote(ref, ref, t_send.at[i - 1], t_recv.at[side], target)

    def s_forward():
        @pl.when(holder)
        def _():
            for w in range(WIN):

                @pl.when(jnp.logical_not(home & (col == w)))
                def _():
                    remote(
                        sown, held.at[w], s_send.at[0], s_recv.at[w], device(c=sibling)
                    ).wait_recv()

            lane = lax.broadcasted_iota(jnp.int32, (16, 128), 1)
            mark = jnp.zeros((16, 128), F32)
            for w in range(WIN):
                sfin[side, w] = held[w, :, 0:F]
                mark = jnp.where(lane == w, held[w, :, F:].astype(F32), mark)
            sfin[side, WIN] = jnp.concatenate([mark, mark], axis=1).astype(BF16)

    def s_spread(e):
        @pl.when(holder & (side == e))
        def _():
            for i in (2, 1, 3):
                t_copy(i).start()

    def s_arrival(e):
        @pl.when(jnp.logical_not(holder & (side == e)))
        def _():
            ref = sfin.at[e]
            remote(ref, ref, t_send.at[0], t_recv.at[e], device(c=sibling)).wait_recv()

    top, bottom = (0, F), (F, F)

    def block(h, w, rows):
        if rows is None:
            return wall.at[h, w]
        return wall.at[h, w, pl.ds(rows[0], rows[1]), :]

    routes = [
        (col, top, upper, lower),
        (col, bottom, lower, upper),
        (col, bottom, upper, lower),
        (col, top, lower, upper),
        (col, None, sibling, sibling),
        (lower, top, upper, far),
        (upper, bottom, lower, far),
        (lower, None, sibling, column(3, 1)),
        (upper, None, sibling, column(1, 1)),
        (far, top, sibling, column(2, 1)),
        (far, bottom, sibling, column(2, 1)),
    ]

    def w_copy(h, index):
        w, rows, target, _ = routes[index]
        ref = block(h, w, rows)
        return remote(ref, ref, w_send.at[h, index], w_recv.at[h, index], device(c=target))

    def w_arrival(h, *indices):
        for index in indices:
            _, rows, _, w = routes[index]
            ref = block(h, w, rows)
            remote(
                ref, ref, w_send.at[h, index], w_recv.at[h, index], device(c=sibling)
            ).wait_recv()

    def w_start(h, *indices):
        for index in indices:
            w_copy(h, index).start()

    def k_copy(i):
        ref = kept.at[col]
        return remote(ref, ref, k_send.at[i - 1], k_recv.at[i - 1], device(c=(col + i) % 8))

    def first_hop(h):
        w_start(h, 0, 1)

    def rest_hop(h):
        w_start(h, 2, 3, 4)

    def second_hop(h):
        w_arrival(h, 0)
        w_start(h, 5)
        w_arrival(h, 1)
        w_start(h, 6)

    def third_hop(h):
        w_arrival(h, 2)
        w_start(h, 7)
        w_arrival(h, 3)
        w_start(h, 8)

    def fourth_hop(h):
        w_arrival(h, 5)
        w_start(h, 9)
        w_arrival(h, 6)
        w_start(h, 10)

    def last_hop(h):
        w_arrival(h, 4, 7, 8, 9, 10)

    def spread_sources(e):
        def body(w, carry):
            rows = jnp.dot(rep[...], sfin[e, w], preferred_element_type=F32)
            spread[e, w] = rows.astype(BF16)
            return carry

        lax.fori_loop(0, WIN, body, 0, unroll=4)

    def count_pairs(e):
        rows = jnp.dot(rep[...], sfin[e, WIN, :, 0:128], preferred_element_type=F32)
        pairs = jnp.dot(rows.astype(BF16), marks[...], preferred_element_type=F32)
        for g in range(2):
            floor = jnp.maximum(pairs[32 * g : 32 * g + 16], 1.0)
            inverse[2 * e + g] = (1.0 / math.sqrt(F)) / floor

    def make(slot, d):
        e, g = d // 2, d % 2
        real_rows = pl.ds(pl.multiple_of(32 * g, 32), 16)
        imag_rows = pl.ds(pl.multiple_of(32 * g + 16, 16), 16)

        def body(w, carry):
            s_real = spread[e, w, real_rows, :]
            s_imag = spread[e, w, imag_rows, :]
            at = pl.multiple_of(w * 2 * F, 2 * F)
            for t in range(ROWS // 16):
                rows = slice(16 * t, 16 * t + 16)
                table = basis[rows, :]
                first, second = (s_real, s_imag) if 2 * t < ROWS // 16 else (-s_imag, s_real)
                tmat[slot, rows, pl.ds(at, F)] = first * table
                tmat[slot, rows, pl.ds(at + F, F)] = second * table
            return carry

        lax.fori_loop(0, WIN, body, 0)

    def partial(p, slot, d):
        cut = slice(p * DP, (p + 1) * DP)
        value = jnp.dot(
            tmat[slot], wall[0, :, :, cut].reshape(WIN * 2 * F, DP), preferred_element_type=F32
        )
        factor = inverse[d, :, cut]
        return (value.reshape(ROWS // 16, 16, DP) * factor[None]).reshape(ROWS, DP)

    up, down, away_day = (day + 1) % 4, (day + 3) % 4, (day + 2) % 4
    head, tail = pl.ds(0, TOP), pl.ds(TOP, ROWS - TOP)

    def d_copy(h, index):
        src, dst, target = [
            (part.at[h, 0, head, :], fold_up.at[h], up),
            (part.at[h, 0, tail, :], fold_down.at[h], down),
            (part.at[h, 1, tail, :], got_up.at[h, tail, :], up),
            (part.at[h, 2, head, :], got_down.at[h, head, :], down),
            (part.at[h, 1, head, :], got_up.at[h, head, :], up),
            (part.at[h, 2, tail, :], got_down.at[h, tail, :], down),
        ][index]
        return remote(src, dst, d_send.at[h, index], d_recv.at[h, index], device(d=target))

    def send_far(h):
        part[h, 0] = partial(h, 0, away_day).astype(BF16)
        d_copy(h, 0).start()
        d_copy(h, 1).start()

    def compute_near(h):
        plus = partial(h, 1, up)
        near[h, 0] = plus
        part[h, 1, TOP:, :] = plus[TOP:].astype(BF16)
        minus = partial(h, 2, down)
        near[h, 1] = minus
        part[h, 2, 0:TOP, :] = minus[:TOP].astype(BF16)

    def send_near(h):
        d_copy(h, 2).start()
        d_copy(h, 3).start()

    def send_folded(h):
        d_copy(h, 0).wait_recv()
        part[h, 1, 0:TOP, :] = (near[h, 0, 0:TOP, :] + fold_up[h].astype(F32)).astype(BF16)
        d_copy(h, 4).start()
        d_copy(h, 1).wait_recv()
        part[h, 2, TOP:, :] = (near[h, 1, TOP:, :] + fold_down[h].astype(F32)).astype(BF16)
        d_copy(h, 5).start()

    def finish(h):
        for index in (2, 3, 4, 5):
            d_copy(h, index).wait_recv()
        result = own[h] + got_up[h].astype(F32) + got_down[h].astype(F32)
        high_part = result.astype(BF16)
        rest_part = (result - high_part.astype(F32)).astype(BF16)
        return [high_part, rest_part, high_part]

    def k_arrival():
        for i in range(1, 8):
            ref = kept.at[(col + 8 - i) % 8]
            remote(ref, ref, k_send.at[i - 1], k_recv.at[i - 1], device(c=sibling)).wait_recv()
        rows = [
            jnp.concatenate([kept[w, 0:1, :], kept[w, 8:9, :]], axis=1).astype(F32)
            for w in range(WIN)
        ]
        marks[0:16, :] = jnp.concatenate(rows + [jnp.zeros((8, CH), F32)]).astype(BF16)

    first_side = away_day // 2
    pl.semaphore_wait(barrier, 7 + 2 + 3 + away.astype(jnp.int32) + 3 * holder.astype(jnp.int32))
    first_hop(0)
    kept[col] = jnp.concatenate(
        [jnp.broadcast_to(keep_row[:, :128], (8, 128)), jnp.broadcast_to(keep_row[:, 128:], (8, 128))]
    ).astype(BF16)
    marks[...] = jnp.zeros_like(marks)

    loads[5].wait()
    picked = jnp.zeros((16, 2 * F), F32)
    for h in range(H):
        picked += lax.dot_general(
            pick[:, h * CP : (h + 1) * CP],
            white[h],
            (((1,), (1,)), ((), ())),
            preferred_element_type=F32,
        )
    lower_half = lax.broadcasted_iota(jnp.int32, (16, F), 0) < 8
    mixed = jnp.where(lower_half, picked[:, :F], picked[:, F:])
    flag = jnp.sum(pick[...].astype(F32) * keep_row, axis=1, keepdims=True)
    message = jnp.concatenate([mixed, jnp.broadcast_to(flag, (16, 128))], axis=1).astype(BF16)
    sown[...] = message

    @pl.when(home)
    def _():
        held[col] = message
    s_each("start")
    for i in range(1, 8):
        k_copy(i).start()
    rest_hop(0)
    second_hop(0)
    s_forward()
    s_spread(first_side)
    third_hop(0)
    s_spread(1 - first_side)
    for copy in loads[6:]:
        copy.wait()
    fourth_hop(0)
    k_arrival()
    s_arrival(first_side)
    spread_sources(first_side)
    make(0, away_day)
    count_pairs(first_side)
    last_hop(0)
    send_far(0)
    send_far(1)
    s_arrival(1 - first_side)
    spread_sources(1 - first_side)
    count_pairs(1 - first_side)
    make(1, up)
    make(2, down)
    compute_near(0)
    send_near(0)
    compute_near(1)
    send_near(1)
    make(3, day)
    own[0] = partial(0, 3, day)
    own[1] = partial(1, 3, day)
    send_folded(0)
    send_folded(1)
    terms = finish(0) + finish(1)
    out[...] = jnp.dot(synth[...], jnp.concatenate(terms), preferred_element_type=F32)

    s_each("wait_send")

    @pl.when(holder)
    def _():
        for i in (1, 2, 3):
            t_copy(i).wait_send()

    for i in range(1, 8):
        k_copy(i).wait_send()
    for h in range(H):
        for index in range(11):
            w_copy(h, index).wait_send()
    for p in range(PARTS):
        for index in range(6):
            d_copy(p, index).wait_send()


def shards(noise, keep):
    samples = noise[0, 0].T
    consts = tables()
    dma = pltpu.SemaphoreType.DMA
    result = pl.pallas_call(
        kernel,
        out_shape=jax.ShapeDtypeStruct((LAGS * PARTS * GROUP, DP), F32),
        in_specs=[
            pl.BlockSpec(memory_space=pltpu.HBM)
            for i in range(2 + len(consts))
        ],
        out_specs=pl.BlockSpec(memory_space=pltpu.VMEM),
        scratch_shapes=[
            pltpu.VMEM(samples.shape, BF16),
            pltpu.VMEM((1, CH), jnp.int32),
            *[pltpu.VMEM(c.shape, BF16) for c in consts],
            dma((2 + len(consts),)),
            pltpu.VMEM((H, WIN, 2 * F, CP), BF16),
            pltpu.VMEM((WIN, 16, 128), BF16),
            pltpu.VMEM((128, CH), BF16),
            pltpu.VMEM((16, SLANES), BF16),
            pltpu.VMEM((WIN, 16, SLANES), BF16),
            pltpu.VMEM((2, WIN + 1, 16, F), BF16),
            pltpu.VMEM((2, WIN, 64, F), BF16),
            pltpu.VMEM((4, ROWS, WIN * 2 * F), BF16),
            pltpu.VMEM((4, 16, CH), F32),
            pltpu.VMEM((PARTS, ROWS, DP), F32),
            pltpu.VMEM((PARTS, 2, ROWS, DP), F32),
            pltpu.VMEM((PARTS, 3, ROWS, DP), BF16),
            pltpu.VMEM((PARTS, TOP, DP), BF16),
            pltpu.VMEM((PARTS, ROWS - TOP, DP), BF16),
            pltpu.VMEM((PARTS, ROWS, DP), BF16),
            pltpu.VMEM((PARTS, ROWS, DP), BF16),
            dma((H, 11)),
            dma((H, 11)),
            dma((7,)),
            dma((7,)),
            dma((4,)),
            dma((WIN,)),
            dma((3,)),
            dma((2,)),
            dma((PARTS, 6)),
            dma((PARTS, 6)),
        ],
        compiler_params=pltpu.CompilerParams(
            collective_id=0, has_side_effects=True, vmem_limit_bytes=60 * 1024 * 1024
        ),
    )(samples, keep[0], *[jnp.asarray(c) for c in consts])
    return result.reshape(LAGS, PARTS, GROUP, DP).transpose(2, 0, 1, 3).reshape(GROUP, LAGS, CH)


def solution(mesh):
    in_specs = (P("day", "col", "row", None), P("day", "col", "row"))
    out_specs = P(("col", "day"), None, "row")
    return jax.shard_map(shards, mesh=mesh, in_specs=in_specs, out_specs=out_specs, check_vma=False)
```

```python
import functools
import math

import jax
import jax.numpy as jnp
import ml_dtypes
import numpy as np
from jax import lax
from jax.experimental import pallas as pl
from jax.experimental.pallas import tpu as pltpu
from jax.sharding import PartitionSpec as P

MESH = pl.DeviceIdType.MESH
BF16 = jnp.bfloat16
F32 = jnp.float32

F = 256
LOW = 60
HALF = 64
MAXLAG = 25
LAGS = 2 * MAXLAG + 1
TLEN = 1500
CH = 256
WIN = 8
GROUP = 4
HALFRANK = 16
RANK = 2 * HALFRANK
ROWS = GROUP * RANK
TOP = ROWS // 2
OUT = 208
SLANES = F + 128
H = 1
CP = CH // H
PARTS = 2
DP = CH // PARTS


def tables():
    k = np.arange(F)
    t = np.arange(TLEN)
    angle = 2.0 * np.pi / TLEN * ((LOW + k)[:, None] * t[None, :] % TLEN)
    twiddle = np.concatenate([np.cos(angle), -np.sin(angle)], axis=0).astype(np.float32)
    high = twiddle.astype(ml_dtypes.bfloat16)
    rest = (twiddle - high.astype(np.float32)).astype(ml_dtypes.bfloat16)
    band = (np.abs(k[:, None] - k[None, :]) <= HALF).astype(ml_dtypes.bfloat16)
    lag = np.arange(LAGS) - MAXLAG
    lag_angle = 2.0 * np.pi / TLEN * ((LOW + k)[None, :] * lag[:, None] % TLEN)
    back, basis = [], []
    for part in (np.cos(lag_angle), -np.sin(lag_angle)):
        left, size, right = np.linalg.svd(part, full_matrices=False)
        left, size, right = left[:, :HALFRANK], size[:HALFRANK], right[:HALFRANK]
        back.append(left * size / 16.0)
        basis.append(right * 16.0)
    basis = np.repeat(np.concatenate(basis), GROUP, axis=0).astype(ml_dtypes.bfloat16)
    synth = np.zeros((OUT, ROWS), np.float32)
    synth[: GROUP * LAGS] = np.kron(np.concatenate(back, axis=1), np.eye(GROUP))
    synth_high = synth.astype(ml_dtypes.bfloat16)
    synth_rest = (synth - synth_high.astype(np.float32)).astype(ml_dtypes.bfloat16)
    terms = np.concatenate([synth_high, synth_high, synth_rest], axis=1)
    synth = np.zeros((LAGS, PARTS, GROUP, PARTS, terms.shape[1]), terms.dtype)
    for p in range(PARTS):
        synth[:, p, :, p] = terms[: GROUP * LAGS].reshape(LAGS, GROUP, -1)
    synth = synth.reshape(LAGS * PARTS * GROUP, -1)
    rep = np.zeros((64, 16), ml_dtypes.bfloat16)
    for g in range(2):
        for part in range(2):
            for i in range(16):
                rep[g * 32 + part * 16 + i, part * 8 + g * GROUP + i % GROUP] = 1
    pick = np.zeros((16, CH), ml_dtypes.bfloat16)
    for i in range(16):
        pick[i, (i % 8) * 32] = 1
    return (
        high,
        rest,
        band,
        basis,
        synth,
        rep,
        pick,
    )


def kernel(
    noise_hbm, keep_hbm, high_hbm, rest_hbm, band_hbm, basis_hbm, synth_hbm, rep_hbm, pick_hbm, out,
    noise, keep, high, rest, band, basis, synth, rep, pick, load,
    wall, kept, marks, sown, held, sfin, spread, tmat, inverse, own, near, part, fold_up, fold_down, got_up, got_down,
    w_send, w_recv, k_send, k_recv, s_send, s_recv, t_send, t_recv, d_send, d_recv,
):
    loads = [
        pltpu.make_async_copy(src, dst, load.at[i])
        for i, (src, dst) in enumerate(
            [
                (noise_hbm, noise),
                (keep_hbm, keep),
                (high_hbm, high),
                (rest_hbm, rest),
                (band_hbm, band),
                (pick_hbm, pick),
                (rep_hbm, rep),
                (basis_hbm, basis),
                (synth_hbm, synth),
            ]
        )
    ]
    for copy in loads[:3]:
        copy.start()

    row, col, day = lax.axis_index("row"), lax.axis_index("col"), lax.axis_index("day")
    z, x = row // 4, row % 4
    y, core = col // 2, col % 2
    side = x % 2
    holder = core == x // 2
    home = jnp.logical_and(holder, y == z)
    away = jnp.logical_not(home)

    def column(step, flip=0):
        return ((y + step) % 4) * 2 + (core + flip) % 2

    upper, lower, far, sibling = column(1), column(3), column(2), column(0, 1)

    def device(r=row, c=col, d=day):
        return (r, c, d)

    def remote(src, dst, send, recv, target):
        return pltpu.make_async_remote_copy(
            src_ref=src, dst_ref=dst, send_sem=send, recv_sem=recv,
            device_id=target, device_id_type=MESH,
        )

    barrier = pltpu.get_barrier_semaphore()

    def greet(target):
        pl.semaphore_signal(barrier, inc=1, device_id=target, device_id_type=MESH)

    for i in range(1, 8):
        greet(device(c=(col + i) % 8))
    for i in (1, 3):
        greet(device(d=(day + i) % 4))
    @pl.when(holder)
    def _():
        for i in range(8):
            if i:
                greet(device(r=4 * y + x, c=(col + i) % 8))
            else:

                @pl.when(away)
                def _():
                    greet(device(r=4 * y + x))

    for e in range(2):

        @pl.when(x != 2 * core + e)
        def _():
            greet(device(r=4 * z + 2 * core + e))

    for copy in loads[3:]:
        copy.start()
    for copy in loads[:3]:
        copy.wait()
    spectrum = jnp.dot(high[...], noise[...], preferred_element_type=F32)
    loads[3].wait()
    spectrum += jnp.dot(rest[...], noise[...], preferred_element_type=F32)
    loads[4].wait()
    keep_row = keep[...].astype(F32)
    bins = lax.broadcasted_iota(jnp.int32, (F, CP), 0)
    count = jnp.minimum(bins + HALF, F - 1) - jnp.maximum(bins - HALF, 0) + 1
    weight = 1.0 / count.astype(F32)

    def whiten(h):
        cut = slice(h * CP, (h + 1) * CP)
        real, imag = spectrum[:F, cut], spectrum[F:, cut]
        magnitude = jnp.sqrt(real * real + imag * imag)
        total = jnp.dot(band[...], magnitude.astype(BF16), preferred_element_type=F32)
        scale = keep_row[:, cut] / (total * weight + 1e-6)
        white = jnp.concatenate([real * scale, imag * scale], axis=0).astype(BF16)
        wall[h, col] = white
        return white

    white = [whiten(0)]
    def s_copy(k):
        target = device(r=((z + k) % 4) * 4 + x, c=row // 2)
        return remote(sown, held.at[col], s_send.at[k], s_recv.at[col], target)

    def s_each(method):
        for k in (1, 2, 3):
            getattr(s_copy(k), method)()

        @pl.when(away)
        def _():
            getattr(s_copy(0), method)()

    def t_copy(i):
        ref = sfin.at[side]
        target = device(r=z * 4 + (x + i) % 4)
        return remote(ref, ref, t_send.at[i - 1], t_recv.at[side], target)

    def s_forward():
        @pl.when(holder)
        def _():
            for w in range(WIN):

                @pl.when(jnp.logical_not(home & (col == w)))
                def _():
                    remote(
                        sown, held.at[w], s_send.at[0], s_recv.at[w], device(c=sibling)
                    ).wait_recv()

            lane = lax.broadcasted_iota(jnp.int32, (16, 128), 1)
            mark = jnp.zeros((16, 128), F32)
            for w in range(WIN):
                sfin[side, w] = held[w, :, 0:F]
                mark = jnp.where(lane == w, held[w, :, F:].astype(F32), mark)
            sfin[side, WIN] = jnp.concatenate([mark, mark], axis=1).astype(BF16)

    def s_spread(e):
        @pl.when(holder & (side == e))
        def _():
            for i in (2, 1, 3):
                t_copy(i).start()

    def s_arrival(e):
        @pl.when(jnp.logical_not(holder & (side == e)))
        def _():
            ref = sfin.at[e]
            remote(ref, ref, t_send.at[0], t_recv.at[e], device(c=sibling)).wait_recv()

    top, bottom = (0, F), (F, F)

    def block(h, w, rows):
        if rows is None:
            return wall.at[h, w]
        return wall.at[h, w, pl.ds(rows[0], rows[1]), :]

    routes = [
        (col, top, upper, lower),
        (col, bottom, lower, upper),
        (col, bottom, upper, lower),
        (col, top, lower, upper),
        (col, None, sibling, sibling),
        (lower, top, upper, far),
        (upper, bottom, lower, far),
        (lower, None, sibling, column(3, 1)),
        (upper, None, sibling, column(1, 1)),
        (far, top, sibling, column(2, 1)),
        (far, bottom, sibling, column(2, 1)),
    ]

    def w_copy(h, index):
        w, rows, target, _ = routes[index]
        ref = block(h, w, rows)
        return remote(ref, ref, w_send.at[h, index], w_recv.at[h, index], device(c=target))

    def w_arrival(h, *indices):
        for index in indices:
            _, rows, _, w = routes[index]
            ref = block(h, w, rows)
            remote(
                ref, ref, w_send.at[h, index], w_recv.at[h, index], device(c=sibling)
            ).wait_recv()

    def w_start(h, *indices):
        for index in indices:
            w_copy(h, index).start()

    def k_copy(i):
        ref = kept.at[col]
        return remote(ref, ref, k_send.at[i - 1], k_recv.at[i - 1], device(c=(col + i) % 8))

    def first_hop(h):
        w_start(h, 0, 1)

    def rest_hop(h):
        w_start(h, 2, 3, 4)

    def second_hop(h):
        w_arrival(h, 0)
        w_start(h, 5)
        w_arrival(h, 1)
        w_start(h, 6)

    def third_hop(h):
        w_arrival(h, 2)
        w_start(h, 7)
        w_arrival(h, 3)
        w_start(h, 8)

    def fourth_hop(h):
        w_arrival(h, 5)
        w_start(h, 9)
        w_arrival(h, 6)
        w_start(h, 10)

    def last_hop(h):
        w_arrival(h, 4, 7, 8, 9, 10)

    def spread_sources(e):
        def body(w, carry):
            rows = jnp.dot(rep[...], sfin[e, w], preferred_element_type=F32)
            spread[e, w] = rows.astype(BF16)
            return carry

        lax.fori_loop(0, WIN, body, 0, unroll=4)

    def count_pairs(e):
        rows = jnp.dot(rep[...], sfin[e, WIN, :, 0:128], preferred_element_type=F32)
        pairs = jnp.dot(rows.astype(BF16), marks[...], preferred_element_type=F32)
        for g in range(2):
            floor = jnp.maximum(pairs[32 * g : 32 * g + 16], 1.0)
            inverse[2 * e + g] = (1.0 / math.sqrt(F)) / floor

    def make(slot, d):
        e, g = d // 2, d % 2
        real_rows = pl.ds(pl.multiple_of(32 * g, 32), 16)
        imag_rows = pl.ds(pl.multiple_of(32 * g + 16, 16), 16)

        def body(w, carry):
            s_real = spread[e, w, real_rows, :]
            s_imag = spread[e, w, imag_rows, :]
            at = pl.multiple_of(w * 2 * F, 2 * F)
            for t in range(ROWS // 16):
                rows = slice(16 * t, 16 * t + 16)
                table = basis[rows, :]
                first, second = (s_real, s_imag) if 2 * t < ROWS // 16 else (-s_imag, s_real)
                tmat[slot, rows, pl.ds(at, F)] = first * table
                tmat[slot, rows, pl.ds(at + F, F)] = second * table
            return carry

        lax.fori_loop(0, WIN, body, 0)

    def partial(p, slot, d):
        cut = slice(p * DP, (p + 1) * DP)
        value = jnp.dot(
            tmat[slot], wall[0, :, :, cut].reshape(WIN * 2 * F, DP), preferred_element_type=F32
        )
        factor = inverse[d, :, cut]
        return (value.reshape(ROWS // 16, 16, DP) * factor[None]).reshape(ROWS, DP)

    up, down, away_day = (day + 1) % 4, (day + 3) % 4, (day + 2) % 4
    head, tail = pl.ds(0, TOP), pl.ds(TOP, ROWS - TOP)

    def d_copy(h, index):
        src, dst, target = [
            (part.at[h, 0, head, :], fold_up.at[h], up),
            (part.at[h, 0, tail, :], fold_down.at[h], down),
            (part.at[h, 1, tail, :], got_up.at[h, tail, :], up),
            (part.at[h, 2, head, :], got_down.at[h, head, :], down),
            (part.at[h, 1, head, :], got_up.at[h, head, :], up),
            (part.at[h, 2, tail, :], got_down.at[h, tail, :], down),
        ][index]
        return remote(src, dst, d_send.at[h, index], d_recv.at[h, index], device(d=target))

    def send_far(h):
        part[h, 0] = partial(h, 0, away_day).astype(BF16)
        d_copy(h, 0).start()
        d_copy(h, 1).start()

    def compute_near(h):
        plus = partial(h, 1, up)
        near[h, 0] = plus
        part[h, 1, TOP:, :] = plus[TOP:].astype(BF16)
        minus = partial(h, 2, down)
        near[h, 1] = minus
        part[h, 2, 0:TOP, :] = minus[:TOP].astype(BF16)

    def send_near(h):
        d_copy(h, 2).start()
        d_copy(h, 3).start()

    def send_folded(h):
        d_copy(h, 0).wait_recv()
        part[h, 1, 0:TOP, :] = (near[h, 0, 0:TOP, :] + fold_up[h].astype(F32)).astype(BF16)
        d_copy(h, 4).start()
        d_copy(h, 1).wait_recv()
        part[h, 2, TOP:, :] = (near[h, 1, TOP:, :] + fold_down[h].astype(F32)).astype(BF16)
        d_copy(h, 5).start()

    def finish(h):
        for index in (2, 3, 4, 5):
            d_copy(h, index).wait_recv()
        result = own[h] + got_up[h].astype(F32) + got_down[h].astype(F32)
        high_part = result.astype(BF16)
        rest_part = (result - high_part.astype(F32)).astype(BF16)
        return [high_part, rest_part, high_part]

    def k_arrival():
        for i in range(1, 8):
            ref = kept.at[(col + 8 - i) % 8]
            remote(ref, ref, k_send.at[i - 1], k_recv.at[i - 1], device(c=sibling)).wait_recv()
        rows = [
            jnp.concatenate([kept[w, 0:1, :], kept[w, 8:9, :]], axis=1).astype(F32)
            for w in range(WIN)
        ]
        marks[0:16, :] = jnp.concatenate(rows + [jnp.zeros((8, CH), F32)]).astype(BF16)

    first_side = away_day // 2
    pl.semaphore_wait(barrier, 7 + 2 + 3 + away.astype(jnp.int32) + 3 * holder.astype(jnp.int32))
    first_hop(0)
    kept[col] = jnp.concatenate(
        [jnp.broadcast_to(keep_row[:, :128], (8, 128)), jnp.broadcast_to(keep_row[:, 128:], (8, 128))]
    ).astype(BF16)
    marks[...] = jnp.zeros_like(marks)

    loads[5].wait()
    picked = jnp.zeros((16, 2 * F), F32)
    for h in range(H):
        picked += lax.dot_general(
            pick[:, h * CP : (h + 1) * CP],
            white[h],
            (((1,), (1,)), ((), ())),
            preferred_element_type=F32,
        )
    lower_half = lax.broadcasted_iota(jnp.int32, (16, F), 0) < 8
    mixed = jnp.where(lower_half, picked[:, :F], picked[:, F:])
    flag = jnp.sum(pick[...].astype(F32) * keep_row, axis=1, keepdims=True)
    message = jnp.concatenate([mixed, jnp.broadcast_to(flag, (16, 128))], axis=1).astype(BF16)
    sown[...] = message

    @pl.when(home)
    def _():
        held[col] = message
    s_each("start")
    for i in range(1, 8):
        k_copy(i).start()
    rest_hop(0)
    second_hop(0)
    s_forward()
    s_spread(first_side)
    third_hop(0)
    s_spread(1 - first_side)
    for copy in loads[6:]:
        copy.wait()
    fourth_hop(0)
    k_arrival()
    s_arrival(first_side)
    spread_sources(first_side)
    make(0, away_day)
    count_pairs(first_side)
    last_hop(0)
    send_far(0)
    send_far(1)
    s_arrival(1 - first_side)
    spread_sources(1 - first_side)
    count_pairs(1 - first_side)
    make(1, up)
    make(2, down)
    compute_near(0)
    send_near(0)
    compute_near(1)
    send_near(1)
    make(3, day)
    own[0] = partial(0, 3, day)
    own[1] = partial(1, 3, day)
    send_folded(0)
    send_folded(1)
    depth = 3 * ROWS
    out[...] = jnp.dot(
        synth[:, 0:depth], jnp.concatenate(finish(0)), preferred_element_type=F32
    )
    out[...] += jnp.dot(
        synth[:, depth:], jnp.concatenate(finish(1)), preferred_element_type=F32
    )

    s_each("wait_send")

    @pl.when(holder)
    def _():
        for i in (1, 2, 3):
            t_copy(i).wait_send()

    for i in range(1, 8):
        k_copy(i).wait_send()
    for h in range(H):
        for index in range(11):
            w_copy(h, index).wait_send()
    for p in range(PARTS):
        for index in range(6):
            d_copy(p, index).wait_send()


def shards(noise, keep):
    samples = noise[0, 0].T
    consts = tables()
    dma = pltpu.SemaphoreType.DMA
    result = pl.pallas_call(
        kernel,
        out_shape=jax.ShapeDtypeStruct((LAGS * PARTS * GROUP, DP), F32),
        in_specs=[
            pl.BlockSpec(memory_space=pltpu.HBM)
            for i in range(2 + len(consts))
        ],
        out_specs=pl.BlockSpec(memory_space=pltpu.VMEM),
        scratch_shapes=[
            pltpu.VMEM(samples.shape, BF16),
            pltpu.VMEM((1, CH), jnp.int32),
            *[pltpu.VMEM(c.shape, BF16) for c in consts],
            dma((2 + len(consts),)),
            pltpu.VMEM((H, WIN, 2 * F, CP), BF16),
            pltpu.VMEM((WIN, 16, 128), BF16),
            pltpu.VMEM((128, CH), BF16),
            pltpu.VMEM((16, SLANES), BF16),
            pltpu.VMEM((WIN, 16, SLANES), BF16),
            pltpu.VMEM((2, WIN + 1, 16, F), BF16),
            pltpu.VMEM((2, WIN, 64, F), BF16),
            pltpu.VMEM((4, ROWS, WIN * 2 * F), BF16),
            pltpu.VMEM((4, 16, CH), F32),
            pltpu.VMEM((PARTS, ROWS, DP), F32),
            pltpu.VMEM((PARTS, 2, ROWS, DP), F32),
            pltpu.VMEM((PARTS, 3, ROWS, DP), BF16),
            pltpu.VMEM((PARTS, TOP, DP), BF16),
            pltpu.VMEM((PARTS, ROWS - TOP, DP), BF16),
            pltpu.VMEM((PARTS, ROWS, DP), BF16),
            pltpu.VMEM((PARTS, ROWS, DP), BF16),
            dma((H, 11)),
            dma((H, 11)),
            dma((7,)),
            dma((7,)),
            dma((4,)),
            dma((WIN,)),
            dma((3,)),
            dma((2,)),
            dma((PARTS, 6)),
            dma((PARTS, 6)),
        ],
        compiler_params=pltpu.CompilerParams(
            collective_id=0, has_side_effects=True, vmem_limit_bytes=60 * 1024 * 1024
        ),
    )(samples, keep[0], *[jnp.asarray(c) for c in consts])
    return result.reshape(LAGS, PARTS, GROUP, DP).transpose(2, 0, 1, 3).reshape(GROUP, LAGS, CH)


def solution(mesh):
    in_specs = (P("day", "col", "row", None), P("day", "col", "row"))
    out_specs = P(("col", "day"), None, "row")
    return jax.shard_map(shards, mesh=mesh, in_specs=in_specs, out_specs=out_specs, check_vma=False)
```
